256 devices in a mesh: ctx: 16 (over y_lo, z), head: 4 (over x), req: 4 (over y_hi, core).
Axes of the slice: x: 4, y: 4 (y_hi: 2, y_lo: 2; y = y_hi * 2 + y_lo), z: 8, core: 2. Of those that a mesh axis runs over, the one named last changes fastest.
Arguments:
- queries: bfloat16 [4, 1024, 4096], P('req', 'ctx', 'head'), may hold values from -6 to 6
- keys: bfloat16 [4, 4096, 1024], P('req', 'ctx', 'head'), may hold values from -6 to 6
- values: bfloat16 [4, 4096, 1024], P('req', 'ctx', 'head'), may hold values from -6 to 6
- grad_out: bfloat16 [4, 1024, 4096], P('req', 'ctx', 'head'), may hold values from -6 to 6
- counts: int32 [4], P('req'), may hold values from 256 to 1024, as said below
- rate_table: float32 [16], replicated, may hold values from -2 to 0
- rate_index: int32 [4, 4096], P('req', 'ctx'), may hold values from 0 to 15
Outputs:
- grad_queries: bfloat16 [4, 1024, 4096], P('req', 'ctx', 'head')
- grad_keys: bfloat16 [4, 4096, 1024], P('req', 'ctx', 'head')
- grad_values: bfloat16 [4, 4096, 1024], P('req', 'ctx', 'head')
- grad_table: float32 [16], replicated
The draws below stay inside these ranges and needn't reach their ends.
Inputs may be any that keep to these rules, and one draw needn't show every extreme that they name: `counts`: some request has exactly 1024 live candidates.
All inputs are finite; a program needn't handle non-finite values.
Results may differ from the reference program's by a relative error of at most 0.022.
Values may be sent and summed in bfloat16 or wider, within the bound.
A program may use at most 64 MiB of HBM per device.

```python
import jax
import jax.numpy as jnp
from jax import lax

QH = 32
KVH = 8
HD = 128
LEVELS = 16
REQS = 4
PREFIX = 4096
CANDS = 1024


def draw_queries(key, part):
    key = jax.random.fold_in(key, 11)
    return jnp.clip(jax.random.normal(key, (REQS, CANDS, QH * HD), jnp.float32), -6.0, 6.0).astype(jnp.bfloat16)


def draw_keys(key, part):
    key = jax.random.fold_in(key, 23)
    return jnp.clip(jax.random.normal(key, (REQS, PREFIX, KVH * HD), jnp.float32), -6.0, 6.0).astype(jnp.bfloat16)


def draw_counts(key, part):
    key = jax.random.fold_in(key, 5)
    first, second = jax.random.split(key)
    base = jax.random.randint(first, (REQS,), CANDS // 4, CANDS + 1)
    full = jax.random.randint(second, (), 0, REQS)
    return jnp.where(jnp.arange(REQS) == full, CANDS, base).astype(jnp.int32)


def plant(drawn, key, smallest, top_value):
    index_at = [jax.random.randint(jax.random.fold_in(key, axis), (), 0, length) for axis, length in enumerate(drawn.shape)]
    longest = drawn.shape.index(max(drawn.shape))
    neighbour = index_at[:longest] + [(index_at[longest] + 1) % drawn.shape[longest]] + index_at[longest + 1:]
    return drawn.at[tuple(index_at)].set(smallest).at[tuple(neighbour)].set(top_value)


def steps_of(key, dims, pieces, least, top_value):
    factor_of, own = 1.0, jax.random.fold_in(key, 6)
    for dim, parts in pieces:
        heights = jnp.exp(jax.random.uniform(jax.random.fold_in(own, dim), (parts,), jnp.float32, least / len(pieces), top_value / len(pieces)))
        factor_of = factor_of * jnp.repeat(heights, dims[dim] // parts).reshape([-1 if axis == dim else 1 for axis in range(len(dims))])
    return factor_of


def normal_values(key, extent, spread, most, pieces=(), kind=jnp.bfloat16):
    values = jax.random.normal(key, extent, jnp.float32) * spread
    if len(pieces) > 0:
        values = steps_of(key, extent, pieces, -0.22, 0.18) * values
    return jnp.clip(values, min=-most, max=most).astype(kind)


def setup_inputs(seed: int = 0) -> dict:
    arg_keys = jax.random.split(jax.random.key(seed), 8)
    return {
        "queries": draw_queries(jax.random.fold_in(arg_keys[7], 71), 0),
        "keys": draw_keys(jax.random.fold_in(arg_keys[7], 71), 0),
        "values": normal_values(arg_keys[2], (REQS, PREFIX, KVH * HD), 1.0, 6.0, ((0, 4), (1, 16), (2, 4))),
        "grad_out": normal_values(arg_keys[3], (REQS, CANDS, QH * HD), 1.0, 6.0, ((0, 4), (1, 16), (2, 4))),
        "counts": draw_counts(jax.random.fold_in(arg_keys[7], 71), 0),
        "rate_table": jnp.clip(jax.random.uniform(arg_keys[5], (LEVELS,), jnp.float32, -2.0, 0.0), -2.0, 0.0),
        "rate_index": plant(jax.random.randint(arg_keys[6], (REQS, PREFIX), 0, LEVELS), jax.random.fold_in(arg_keys[6], 1), 0, LEVELS - 1).astype(jnp.int32),
    }


score_scale = 128.0 ** -0.5


def barrier_round(value):
    return lax.optimization_barrier(value.astype(jnp.bfloat16)).astype(jnp.float32)


def request_grads(query_rows, key_rows, value_rows, masked, bias):
    group = QH // KVH
    q_heads = jnp.transpose(query_rows.reshape(CANDS, KVH, group, HD), (1, 2, 0, 3))
    o_heads = jnp.transpose(masked.reshape(CANDS, KVH, group, HD), (1, 2, 0, 3))
    k_heads = jnp.transpose(key_rows.reshape(PREFIX, KVH, HD), (1, 0, 2))
    v_heads = jnp.transpose(value_rows.reshape(PREFIX, KVH, HD), (1, 0, 2))
    bias_f = bias.astype(jnp.float32)
    high = lax.Precision.HIGHEST

    def one_group(inputs):
        q_g, k_g, v_g, o_g = inputs
        qf = q_g.astype(jnp.float32)
        kf = k_g.astype(jnp.float32)
        vf = v_g.astype(jnp.float32)
        of = o_g.astype(jnp.float32)
        scores = jnp.einsum('jcd,pd->jcp', qf, kf, precision=high) * score_scale + bias_f
        lse = jax.nn.logsumexp(scores, axis=-1)
        prob = jnp.exp(scores - lse[..., None])
        out = jnp.einsum('jcp,pd->jcd', prob, vf, precision=high)
        delta = jnp.sum(of * out, axis=-1)
        dprob = jnp.einsum('jcd,pd->jcp', of, vf, precision=high)
        dscore = prob * (dprob - delta[..., None])
        prob_b = barrier_round(prob)
        dscore_b = barrier_round(dscore)
        grad_v = jnp.einsum('jcp,jcd->pd', prob_b, of, precision=high)
        grad_k = jnp.einsum('jcp,jcd->pd', dscore_b, qf, precision=high) * score_scale
        grad_q = jnp.einsum('jcp,pd->jcd', dscore_b, kf, precision=high) * score_scale
        column = jnp.sum(dscore, axis=(0, 1))
        return grad_q, grad_k, grad_v, column

    grad_q, grad_k, grad_v, column = lax.map(one_group, (q_heads, k_heads, v_heads, o_heads))
    grad_q = jnp.transpose(grad_q, (2, 0, 1, 3)).reshape(CANDS, QH * HD)
    grad_k = jnp.transpose(grad_k, (1, 0, 2)).reshape(PREFIX, KVH * HD)
    grad_v = jnp.transpose(grad_v, (1, 0, 2)).reshape(PREFIX, KVH * HD)
    return grad_q, grad_k, grad_v, jnp.sum(column, axis=0)


def reference(queries, keys, values, grad_out, counts, rate_table, rate_index):
    q_list, k_list, v_list = [], [], []
    grad_table = jnp.zeros((LEVELS,), jnp.float32)
    slots = jnp.arange(CANDS, dtype=jnp.int32)
    for request in range(REQS):
        live = slots < counts[request]
        masked = jnp.where(live[:, None], grad_out[request], jnp.zeros_like(grad_out[request]))
        bias = rate_table[rate_index[request]].astype(jnp.bfloat16)
        grad_q, grad_k, grad_v, column = request_grads(queries[request], keys[request], values[request], masked, bias)
        q_list.append(grad_q.astype(jnp.bfloat16))
        k_list.append(grad_k.astype(jnp.bfloat16))
        v_list.append(grad_v.astype(jnp.bfloat16))
        grad_table = grad_table + jax.ops.segment_sum(column, rate_index[request], num_segments=LEVELS)
    return jnp.stack(q_list), jnp.stack(k_list), jnp.stack(v_list), grad_table
```

```python
import functools

import jax
import jax.numpy as jnp
from jax import lax
from jax.experimental import pallas as pl
from jax.experimental.pallas import tpu as pltpu
from jax.sharding import PartitionSpec as P

HD = 128
Z = 8
SCALE = 128.0 ** (-0.5)
LOG2E = 1.4426950408889634
MESH = pl.DeviceIdType.MESH
F32 = jnp.float32
BF16 = jnp.bfloat16
NT = (((1,), (1,)), ((), ()))
TN = (((0,), (0,)), ((), ()))
NN = (((1,), (0,)), ((), ()))


def kernel(
    n_head, n_req, cand, pre, group, kv, levels,
    counts_ref, table_ref, index_ref, q_hbm, k_hbm, v_hbm, o_hbm,
    dq_hbm, dk_hbm, dv_hbm, dt_ref,
    qo, ks, vs, kt, idx_par, bias, onehot,
    probs, dprobs, peaks, st_loc, st_in, st_fin, st_out,
    dq_tmp, rs_out, rs_in, dq_done, dk_acc, dv_acc, col, kv_out, kv_in, kv_done,
    t_loc, t_in1, t_in2, t_in3, t_mid,
    in_sem, out_sem, kv_send, kv_recv, ix_send, ix_recv,
    ag_send, ag_recv, sa_send, sa_recv, sb_send, sb_recv,
    rs_send, rs_recv, dk_send, dk_recv,
    t1_send, t1_recv, t2_send, t2_recv, t3_send, t3_recv,
):
    rows = group * cand
    half = rows // 2
    lanes = rows // HD
    ctx = lax.axis_index("ctx")
    head = lax.axis_index("head")
    req = lax.axis_index("req")
    y = ctx // Z
    z = ctx % Z

    def along_z(by):
        return {"ctx": y * Z + (z + by) % Z}

    partner = {"ctx": (1 - y) * Z + z}
    right, left = along_z(1), along_z(Z - 1)
    t2_codes = [(a, b) for a in range(2) for b in range(n_req) if (a, b) != (0, 0)]

    def t2_peer(a, b):
        return {"ctx": ((y + a) % 2) * Z + z, "req": (req + b) % n_req}

    def t3_peer(b):
        return {"head": (head + b) % n_head}

    loads = []
    for g in range(kv):
        for j in range(group):
            lo = (g * group + j) * HD
            for part, src in ((0, q_hbm), (1, o_hbm)):
                loads.append(pltpu.make_async_copy(
                    src.at[0, :, pl.ds(lo, HD)],
                    qo.at[0, g, part, pl.ds(j * cand, cand), :],
                    in_sem.at[len(loads)]))
        for src, dst in ((k_hbm, ks), (v_hbm, vs)):
            loads.append(pltpu.make_async_copy(
                src.at[0, :, pl.ds(g * HD, HD)],
                dst.at[g, pl.ds(0, pre), :],
                in_sem.at[len(loads)]))
    for copy in loads:
        copy.start()

    barrier = pltpu.get_barrier_semaphore()
    peers = [along_z(o) for o in range(1, Z)]
    peers += [t2_peer(a, b) for a, b in t2_codes]
    peers += [t3_peer(b) for b in range(1, n_head)]
    for peer in peers:
        pl.semaphore_signal(barrier, inc=1, device_id=peer, device_id_type=MESH)

    rs_in[:, :, 0] = jnp.zeros_like(rs_in[:, :, 0])
    dk_acc[...] = jnp.zeros_like(dk_acc)
    dv_acc[...] = jnp.zeros_like(dv_acc)
    col[...] = jnp.zeros_like(col)

    for copy in loads:
        copy.wait()
    live = counts_ref[0] - ctx * cand
    slot = lax.rem(lax.broadcasted_iota(jnp.int32, (rows, HD), 0), cand)
    for g in range(kv):
        qo[0, g, 1] = jnp.where(slot < live, qo[0, g, 1], jnp.zeros((rows, HD), BF16))

    pl.semaphore_wait(barrier, len(peers))

    def remote(src, dst, send, recv, device):
        return pltpu.make_async_remote_copy(
            src_ref=src, dst_ref=dst, send_sem=send, recv_sem=recv,
            device_id=device, device_id_type=MESH)

    def gather(g, way, step, part):
        if way == 0:
            src, dst, device = lax.rem(9 - step, Z), Z - step, right
        else:
            src, dst, device = step - 1, step, left
        return remote(
            qo.at[src, g, part], qo.at[dst, g, part],
            ag_send.at[g, way, part, step - 1], ag_recv.at[g, way, part, step - 1], device)

    def kv_copy(g, which):
        ref = (ks, vs)[which]
        return remote(
            ref.at[g, pl.ds(0, pre), :], ref.at[g, pl.ds(pre, pre), :],
            kv_send.at[g, which], kv_recv.at[g, which], partner)

    ix_copy = remote(index_ref, idx_par, ix_send, ix_recv, partner)

    def stat_a(g, o):
        return remote(
            st_loc.at[g, o], st_in.at[g, o],
            sa_send.at[g, o], sa_recv.at[g, o], along_z(o))

    def stat_b(g, o):
        return remote(
            st_out.at[g], st_fin.at[g, Z - o],
            sb_send.at[g, o], sb_recv.at[g, o], along_z(o))

    def scatter_half(g, way):
        at = pl.ds(way * half, half)
        return remote(
            rs_out.at[g, way, 0, at, :], rs_in.at[g, way, 0, at, :],
            rs_send.at[g, way, 0], rs_recv.at[g, way, 0], (left, right)[way])

    def scatter(g, way, step):
        return remote(
            rs_out.at[g, way, step], rs_in.at[g, way, step],
            rs_send.at[g, way, step], rs_recv.at[g, way, step], (left, right)[way])

    def kv_grad(g, which):
        return remote(
            kv_out.at[g, which], kv_in.at[g, which],
            dk_send.at[g, which], dk_recv.at[g, which], partner)

    def t1_copy(o):
        return remote(t_loc, t_in1.at[o], t1_send.at[o], t1_recv.at[o], along_z(o))

    def t2_copy(i):
        return remote(
            t_mid.at[0], t_in2.at[i], t2_send.at[i], t2_recv.at[i], t2_peer(*t2_codes[i]))

    def t3_copy(b):
        return remote(t_mid.at[1], t_in3.at[b], t3_send.at[b], t3_recv.at[b], t3_peer(b))

    ix_copy.start()
    for g in range(kv):
        for which in range(2):
            kv_copy(g, which).start()
    for part in range(2):
        for way in range(2):
            gather(0, way, 1, part).start()

    level = lax.broadcasted_iota(jnp.int32, (levels, HD), 0)
    table = jnp.zeros((levels, HD), F32)
    for i in range(levels):
        table = jnp.where(level == i, table_ref[i], table)
    table = table.astype(BF16)

    def offsets(index, place):
        hot = (lax.broadcasted_iota(jnp.int32, (levels, pre), 0) == index).astype(F32)
        onehot[place] = hot
        bias[pl.ds(place * pre, pre), :] = lax.dot_general(
            hot.astype(BF16), table, TN, preferred_element_type=F32) * LOG2E

    offsets(index_ref[...], 0)
    ix_copy.wait()
    offsets(idx_par[...], 1)

    def split(row):
        return [row[:, i * HD:(i + 1) * HD] for i in range(lanes)]

    def first_pass(g, s):
        q_blk = qo[s, g, 0]
        o_blk = qo[s, g, 1]
        off = jnp.concatenate([bias[...]] * lanes, axis=1)
        scores = lax.dot_general(ks[g], q_blk, NT, preferred_element_type=F32)
        scores = scores * (SCALE * LOG2E) + off
        peak = jnp.max(scores, axis=0, keepdims=True)
        prob = jnp.exp2(scores - peak)
        total = jnp.sum(prob, axis=0, keepdims=True)
        dprob = lax.dot_general(vs[g], o_blk, NT, preferred_element_type=F32)
        delta = jnp.sum(prob * dprob, axis=0, keepdims=True) / total
        probs[g, s] = prob
        dprobs[g, s] = dprob
        peaks[g, s] = peak
        lse = peak + jnp.log2(total)
        st_loc[g, s] = jnp.concatenate(split(lse) + split(delta), axis=0)

    def combine(g):
        st_in[g, 0] = st_loc[g, 0]
        parts = st_in[g]
        lse = parts[:, 0:lanes]
        top = jnp.max(lse, axis=0, keepdims=True)
        total = top + jnp.log2(jnp.sum(jnp.exp2(lse - top), axis=0, keepdims=True))
        weight = jnp.exp2(lse - total)
        delta = jnp.sum(weight * parts[:, lanes:], axis=0)
        both = jnp.concatenate([total[0], delta], axis=0)
        st_out[g] = both
        st_fin[g, 0] = both

    def second_pass(g, s, c):
        fin = st_fin[g, s]
        lse = jnp.concatenate([fin[i:i + 1] for i in range(lanes)], axis=1)
        delta = jnp.concatenate([fin[lanes + i:lanes + i + 1] for i in range(lanes)], axis=1)
        prob = probs[g, s] * jnp.exp2(peaks[g, s] - lse)
        dscore = prob * (dprobs[g, s] - delta)
        col[...] += functools.reduce(lambda a, b: a + b, split(dscore))
        prob_b = prob.astype(BF16)
        dscore_b = dscore.astype(BF16)
        dv_acc[g] += lax.dot_general(prob_b, qo[s, g, 1], NN, preferred_element_type=F32)
        dk_acc[g] += lax.dot_general(dscore_b, qo[s, g, 0], NN, preferred_element_type=F32)
        dq = lax.dot_general(kt[g], dscore_b, NN, preferred_element_type=F32)
        dq_tmp[c] = dq.T

    def kv_finish(g):
        for which, acc, hbm in ((0, dk_acc, dk_hbm), (1, dv_acc, dv_hbm)):
            kv_grad(g, which).wait_recv()
            total = acc[g, 0:pre] + kv_in[g, which].astype(F32)
            if which == 0:
                total = total * SCALE
            kv_done[g, which] = total.astype(BF16)

    def kv_store(g, which):
        hbm = (dk_hbm, dv_hbm)[which]
        return pltpu.make_async_copy(
            kv_done.at[g, which], hbm.at[0, :, pl.ds(g * HD, HD)], out_sem.at[g, which])

    def dq_store(g, j):
        return pltpu.make_async_copy(
            dq_done.at[g, pl.ds(j * cand, cand), :],
            dq_hbm.at[0, :, pl.ds((g * group + j) * HD, HD)],
            out_sem.at[g, 2 + j])

    def tick(t, _):
        phase, k = t // 6, t % 6

        for g in range(kv):
            @pl.when((phase == g) & (k == 0))
            def _():
                if g > 0:
                    for part in range(2):
                        for way in range(2):
                            gather(g, way, 1, part).start()
                for which in range(2):
                    kv_copy(g, which).wait()
                kt[g] = ks[g].astype(F32).T.astype(BF16)

        @pl.when((phase < kv) & (k >= 1) & (k < 4))
        def _():
            for part in range(2):
                for way in range(2):
                    gather(phase, way, k, part).wait_recv()

                    @pl.when((k < 3) | (part == way))
                    def _():
                        gather(phase, way, k + 1, part).start()

        @pl.when((phase < kv) & (k == 4))
        def _():
            gather(phase, 0, 4, 0).wait_recv()
            gather(phase, 1, 4, 1).wait_recv()

        @pl.when((phase < kv) & (k < 5))
        def _():
            def chunk(c, _):
                s = jnp.where(c == 0, (Z - k) % Z, k)
                first_pass(phase, s)
                return 0

            lax.fori_loop(0, jnp.where((k == 0) | (k == 4), 1, 2), chunk, 0)

            @pl.when(k == 4)
            def _():
                for o in range(1, Z):
                    stat_a(phase, o).start()

        h = phase - 1

        @pl.when((phase > 0) & (k == 0))
        def _():
            for o in range(1, Z):
                stat_a(h, o).wait()
            combine(h)
            for o in range(1, Z):
                stat_b(h, o).start()

        @pl.when((phase > 0) & (k > 0))
        def _():
            j = k - 1

            @pl.when(j == 0)
            def _():
                for o in range(1, Z):
                    stat_b(h, o).wait()

            def chunk(c, _):
                s = jnp.where(c == 0, (4 + j) % Z, 4 - j)
                second_pass(h, s, c)

                @pl.when(j == 0)
                def _():
                    for way in range(2):
                        at = pl.ds(way * half, half)
                        rs_out[h, way, 0, at, :] = dq_tmp[0, at, :].astype(BF16)
                        scatter_half(h, way).start()

                for way in range(2):
                    @pl.when((j > 0) & (j < 4) & (c == way))
                    def _():
                        @pl.when(j == 1)
                        def _():
                            scatter_half(h, way).wait_recv()

                        @pl.when(j > 1)
                        def _():
                            scatter(h, way, j - 1).wait_recv()

                        rs_out[h, way, j] = (
                            dq_tmp[way] + rs_in[h, way, j - 1].astype(F32)).astype(BF16)
                        scatter(h, way, j).start()
                return 0

            lax.fori_loop(0, jnp.where((j == 0) | (j == 4), 1, 2), chunk, 0)

            @pl.when(j == 4)
            def _():
                for which, acc in ((0, dk_acc), (1, dv_acc)):
                    kv_out[h, which] = acc[h, pre:2 * pre].astype(BF16)
                    kv_grad(h, which).start()

                @pl.when(phase == kv)
                def _():
                    t_loc[...] = sum(
                        lax.dot_general(
                            onehot[i], col[i * pre:(i + 1) * pre], NN,
                            precision=lax.Precision.HIGHEST, preferred_element_type=F32)
                        for i in range(2))
                    for o in range(1, Z):
                        t1_copy(o).start()

                for way in range(2):
                    scatter(h, way, 3).wait_recv()
                dq = dq_tmp[0] + rs_in[h, 0, 3].astype(F32) + rs_in[h, 1, 3].astype(F32)
                dq_done[h] = (dq * SCALE).astype(BF16)

        for g in range(kv):
            @pl.when((phase == g + 1) & (k == 5))
            def _():
                for j in range(group):
                    dq_store(g, j).start()
        return 0

    lax.fori_loop(0, 6 * (kv + 1), tick, 0)

    for o in range(1, Z):
        t1_copy(o).wait()
    t_mid[0] = t_loc[...] + sum(t_in1[o] for o in range(1, Z))
    for i in range(len(t2_codes)):
        t2_copy(i).start()
    for g in range(kv):
        kv_finish(g)
        for which in range(2):
            kv_store(g, which).start()
    for i in range(len(t2_codes)):
        t2_copy(i).wait()
    total = t_mid[0] + sum(t_in2[i] for i in range(len(t2_codes)))
    if n_head > 1:
        t_mid[1] = total
        for b in range(1, n_head):
            t3_copy(b).start()

    for g in range(kv):
        for way in range(2):
            for part in range(2):
                for step in range(1, 5):
                    if step < 4 or part == way:
                        gather(g, way, step, part).wait_send()
            scatter_half(g, way).wait_send()
            for step in range(1, 4):
                scatter(g, way, step).wait_send()
        for which in range(2):
            kv_grad(g, which).wait_send()
            kv_store(g, which).wait()
        for j in range(group):
            dq_store(g, j).wait()

    if n_head > 1:
        for b in range(1, n_head):
            t3_copy(b).wait()
        total = total + sum(t_in3[b] for b in range(1, n_head))
    total = jnp.sum(total, axis=1, keepdims=True)
    place = lax.broadcasted_iota(jnp.int32, (levels, levels), 0)
    across = lax.broadcasted_iota(jnp.int32, (levels, levels), 1)
    dt_ref[...] = jnp.sum(
        jnp.where(place == across, total, 0.0), axis=0, keepdims=True)


def shards(queries, keys, values, grad_out, counts, rate_table, rate_index):
    n_head, n_req = lax.axis_size("head"), lax.axis_size("req")
    cand, pre = queries.shape[1], keys.shape[1]
    kv = keys.shape[2] // HD
    group = queries.shape[2] // keys.shape[2]
    levels = rate_table.shape[0]
    rows = group * cand
    lanes = rows // HD
    any_ = pl.BlockSpec(memory_space=pl.ANY)
    smem = pl.BlockSpec(memory_space=pltpu.SMEM)
    vmem = pl.BlockSpec(memory_space=pltpu.VMEM)
    dma = pltpu.SemaphoreType.DMA
    out = pl.pallas_call(
        functools.partial(kernel, n_head, n_req, cand, pre, group, kv, levels),
        out_shape=(
            jax.ShapeDtypeStruct(queries.shape, BF16),
            jax.ShapeDtypeStruct(keys.shape, BF16),
            jax.ShapeDtypeStruct(values.shape, BF16),
            jax.ShapeDtypeStruct((1, levels), F32),
        ),
        in_specs=[smem, smem, vmem, any_, any_, any_, any_],
        out_specs=(any_, any_, any_, vmem),
        scratch_shapes=[
            pltpu.VMEM((Z, kv, 2, rows, HD), BF16),
            pltpu.VMEM((kv, 2 * pre, HD), BF16),
            pltpu.VMEM((kv, 2 * pre, HD), BF16),
            pltpu.VMEM((kv, HD, 2 * pre), BF16),
            pltpu.VMEM((1, pre), jnp.int32),
            pltpu.VMEM((2 * pre, HD), F32),
            pltpu.VMEM((2, levels, pre), F32),
            pltpu.VMEM((kv, Z, 2 * pre, rows), F32),
            pltpu.VMEM((kv, Z, 2 * pre, rows), F32),
            pltpu.VMEM((kv, Z, 1, rows), F32),
            pltpu.VMEM((kv, Z, 2 * lanes, HD), F32),
            pltpu.VMEM((kv, Z, 2 * lanes, HD), F32),
            pltpu.VMEM((kv, Z, 2 * lanes, HD), F32),
            pltpu.VMEM((kv, 2 * lanes, HD), F32),
            pltpu.VMEM((2, rows, HD), F32),
            pltpu.VMEM((kv, 2, 4, rows, HD), BF16),
            pltpu.VMEM((kv, 2, 4, rows, HD), BF16),
            pltpu.VMEM((kv, rows, HD), BF16),
            pltpu.VMEM((kv, 2 * pre, HD), F32),
            pltpu.VMEM((kv, 2 * pre, HD), F32),
            pltpu.VMEM((2 * pre, HD), F32),
            pltpu.VMEM((kv, 2, pre, HD), BF16),
            pltpu.VMEM((kv, 2, pre, HD), BF16),
            pltpu.VMEM((kv, 2, pre, HD), BF16),
            pltpu.VMEM((levels, HD), F32),
            pltpu.VMEM((Z, levels, HD), F32),
            pltpu.VMEM((2 * n_req - 1, levels, HD), F32),
            pltpu.VMEM((n_head, levels, HD), F32),
            pltpu.VMEM((2, levels, HD), F32),
            dma((kv * (2 * group + 2),)),
            dma((kv, 2 + group)),
            dma((kv, 2)),
            dma((kv, 2)),
            dma,
            dma,
            dma((kv, 2, 2, 4)),
            dma((kv, 2, 2, 4)),
            dma((kv, Z)),
            dma((kv, Z)),
            dma((kv, Z)),
            dma((kv, Z)),
            dma((kv, 2, 4)),
            dma((kv, 2, 4)),
            dma((kv, 2)),
            dma((kv, 2)),
            dma((Z,)),
            dma((Z,)),
            dma((2 * n_req - 1,)),
            dma((2 * n_req - 1,)),
            dma((n_head,)),
            dma((n_head,)),
        ],
        compiler_params=pltpu.CompilerParams(
            collective_id=0, has_side_effects=True, vmem_limit_bytes=48 * 1024 * 1024),
    )(counts, rate_table, rate_index, queries, keys, values, grad_out)
    return out[0], out[1], out[2], out[3].reshape(levels)


def solution(mesh):
    split = P("req", "ctx", "head")
    return jax.shard_map(
        shards,
        mesh=mesh,
        in_specs=(split, split, split, split, P("req"), P(), P("req", "ctx")),
        out_specs=(split, split, split, P()),
        check_vma=False,
    )
```

```python
import functools

import jax
import jax.numpy as jnp
from jax import lax
from jax.experimental import pallas as pl
from jax.experimental.pallas import tpu as pltpu
from jax.sharding import PartitionSpec as P

HD = 128
Z = 8
SCALE = 128.0 ** (-0.5)
LOG2E = 1.4426950408889634
MESH = pl.DeviceIdType.MESH
F32 = jnp.float32
BF16 = jnp.bfloat16
NT = (((1,), (1,)), ((), ()))
TN = (((0,), (0,)), ((), ()))
NN = (((1,), (0,)), ((), ()))


def kernel(
    n_head, n_req, cand, pre, group, kv, levels,
    counts_ref, table_ref, index_ref, q_hbm, k_hbm, v_hbm, o_hbm,
    dq_hbm, dk_hbm, dv_hbm, dt_ref,
    qo, ks, vs, kt, idx_par, bias, onehot,
    probs, dprobs, peaks, deltas, fin, lev_a, lev_b, st_loc, st_in, st_all,
    dq_all, rs_out, rs_in, dq_done, dk_acc, dv_acc, kv_out, kv_in, kv_done,
    t_mid, t_in1, t_in2,
    in_sem, out_sem, kv_send, kv_recv, ix_send, ix_recv,
    ag_send, ag_recv, sa_send, sa_recv, sb_send, sb_recv,
    rs_send, rs_recv, dk_send, dk_recv,
    t1_send, t1_recv, t2_send, t2_recv,
):
    rows = group * cand
    half = rows // 2
    lanes = rows // HD
    n_core = min(n_req, 2)
    n_hi = n_req // n_core
    ctx = lax.axis_index("ctx")
    head = lax.axis_index("head")
    req = lax.axis_index("req")
    y = ctx // Z
    z = ctx % Z
    hi = req // n_core
    core = req % n_core

    def along_z(by):
        return {"ctx": y * Z + (z + by) % Z}

    partner = {"ctx": (1 - y) * Z + z}
    right, left = along_z(1), along_z(Z - 1)
    t1_codes = [(a, b) for a in range(Z) for b in range(n_core)][1:]
    t2_codes = [
        (a, b, c) for a in range(n_head) for b in range(2) for c in range(n_hi)][1:]

    def t1_peer(a, b):
        return {"ctx": y * Z + (z + a) % Z, "req": hi * n_core + (core + b) % n_core}

    def t2_peer(a, b, c):
        return {
            "head": (head + a) % n_head,
            "ctx": ((y + b) % 2) * Z + z,
            "req": ((hi + c) % n_hi) * n_core + core,
        }

    barrier = pltpu.get_barrier_semaphore()
    peers = [t1_peer(*code) for code in t1_codes] + [t2_peer(*code) for code in t2_codes]
    for peer in peers:
        pl.semaphore_signal(barrier, inc=1, device_id=peer, device_id_type=MESH)

    loads, late_loads = [], []
    for g in range(kv):
        for j in range(group):
            lo = (g * group + j) * HD
            for part, src in ((0, q_hbm), (1, o_hbm)):
                loads.append(pltpu.make_async_copy(
                    src.at[0, :, pl.ds(lo, HD)],
                    qo.at[0, g, part, pl.ds(j * cand, cand), :],
                    in_sem.at[len(loads)]))
    for g in range(kv):
        for src, dst in ((k_hbm, ks), (v_hbm, vs)):
            late_loads.append(pltpu.make_async_copy(
                src.at[0, :, pl.ds(g * HD, HD)],
                dst.at[g, pl.ds(0, pre), :],
                in_sem.at[len(loads) + len(late_loads)]))
    for copy in loads + late_loads:
        copy.start()

    rs_in[:, :, 0] = jnp.zeros_like(rs_in[:, :, 0])
    dk_acc[...] = jnp.zeros_like(dk_acc)
    dv_acc[...] = jnp.zeros_like(dv_acc)

    level = lax.broadcasted_iota(jnp.int32, (levels, HD), 0)
    table = jnp.zeros((levels, HD), F32)
    for i in range(levels):
        table = jnp.where(level == i, table_ref[i], table)
    table = table.astype(BF16)

    def offsets(index, place):
        hot = (lax.broadcasted_iota(jnp.int32, (levels, pre), 0) == index)
        hot = hot.astype(F32).astype(BF16)
        onehot[:, pl.ds(place * pre, pre)] = hot
        bias[pl.ds(place * pre, pre), :] = lax.dot_general(
            hot, table, TN, preferred_element_type=F32) * LOG2E

    offsets(index_ref[...], 0)

    for copy in loads + late_loads:
        copy.wait()
    live = counts_ref[0] - ctx * cand
    slot = lax.rem(lax.broadcasted_iota(jnp.int32, (rows, HD), 0), cand)
    for g in range(kv):
        qo[0, g, 1] = jnp.where(slot < live, qo[0, g, 1], jnp.zeros((rows, HD), BF16))

    pl.semaphore_wait(barrier, len(peers))

    def remote(src, dst, send, recv, device):
        return pltpu.make_async_remote_copy(
            src_ref=src, dst_ref=dst, send_sem=send, recv_sem=recv,
            device_id=device, device_id_type=MESH)

    def gather(g, way, step, part):
        if way == 0:
            src, dst, device = lax.rem(9 - step, Z), Z - step, right
        else:
            src, dst, device = step - 1, step, left
        return remote(
            qo.at[src, g, part], qo.at[dst, g, part],
            ag_send.at[g, way, part, step - 1], ag_recv.at[g, way, part, step - 1], device)

    def kv_copy(g, which):
        ref = (ks, vs)[which]
        return remote(
            ref.at[g, pl.ds(0, pre), :], ref.at[g, pl.ds(pre, pre), :],
            kv_send.at[g, which], kv_recv.at[g, which], partner)

    ix_copy = remote(index_ref, idx_par, ix_send, ix_recv, partner)

    def stat_a(g, o):
        return remote(
            st_loc.at[g, o], st_in.at[g, o],
            sa_send.at[g, o], sa_recv.at[g, o], along_z(o))

    def stat_b(g, o):
        return remote(
            st_all.at[g, 0], st_all.at[g, o],
            sb_send.at[g, o], sb_recv.at[g, o], along_z(o))

    def scatter(g, way, step, part):
        at = pl.ds(part * half, half)
        return remote(
            rs_out.at[g, way, step, at, :], rs_in.at[g, way, step, at, :],
            rs_send.at[g, way, step, part], rs_recv.at[g, way, step, part],
            (left, right)[way])

    def kv_grad(g, which):
        return remote(
            kv_out.at[g, which], kv_in.at[g, which],
            dk_send.at[g, which], dk_recv.at[g, which], partner)

    def t1_copy(i):
        return remote(
            t_mid.at[0], t_in1.at[i], t1_send.at[i], t1_recv.at[i], t1_peer(*t1_codes[i]))

    def t2_copy(i):
        return remote(
            t_mid.at[1], t_in2.at[i], t2_send.at[i], t2_recv.at[i], t2_peer(*t2_codes[i]))

    for g in range(kv):
        for part in range(2):
            for way in range(2):
                gather(g, way, 1, part).start()
        if g == 0:
            ix_copy.start()
        for which in range(2):
            kv_copy(g, which).start()

    ix_copy.wait()
    offsets(idx_par[...], 1)

    def split(row):
        return [row[:, i * HD:(i + 1) * HD] for i in range(lanes)]

    def joined(block):
        return jnp.concatenate([block[i:i + 1] for i in range(lanes)], axis=1)

    def first_pass(g, s):
        q_blk = qo[s, g, 0]
        o_blk = qo[s, g, 1]
        off = jnp.concatenate([bias[...]] * lanes, axis=1)
        scores = lax.dot_general(ks[g], q_blk, NT, preferred_element_type=F32)
        scores = scores * (SCALE * LOG2E) + off
        peak = jnp.max(scores, axis=0, keepdims=True)
        prob = jnp.exp2(scores - peak)
        total = jnp.sum(prob, axis=0, keepdims=True)
        dprob = lax.dot_general(vs[g], o_blk, NT, preferred_element_type=F32)
        delta = jnp.sum(prob * dprob, axis=0, keepdims=True) / total
        probs[g, s] = prob
        dprobs[g, s] = dprob
        peaks[g, s] = peak
        deltas[g, s] = delta
        lev_a[g, s] = lax.dot_general(
            onehot[...], (prob * (dprob - delta)).astype(BF16), NN,
            preferred_element_type=F32)
        lev_b[g, s] = lax.dot_general(
            onehot[...], prob.astype(BF16), NN, preferred_element_type=F32)
        lse = peak + jnp.log2(total)
        st_loc[g, s] = jnp.concatenate(split(lse) + split(delta), axis=0)

    def merged(parts):
        lse = [p[0:lanes] for p in parts]
        top = functools.reduce(jnp.maximum, lse)
        total = top + jnp.log2(sum(jnp.exp2(v - top) for v in lse))
        delta = sum(jnp.exp2(v - total) * p[lanes:] for v, p in zip(lse, parts))
        return total, delta

    def combine(g):
        total, delta = merged([st_loc[g, 0]] + [st_in[g, o] for o in range(1, Z) if o != 4])
        st_all[g, 0, 0] = jnp.concatenate([total, delta], axis=0)

    def finish(g):
        def one(s, acc):
            total, delta = merged([
                st_all[g, lax.rem(Z - s, Z), 0], st_all[g, lax.rem(12 - s, Z), 1]])
            delta = joined(delta)
            factor = jnp.exp2(peaks[g, s] - joined(total))
            fin[g, s] = jnp.concatenate([factor, delta], axis=0)
            term = factor * (lev_a[g, s] - (delta - deltas[g, s]) * lev_b[g, s])
            return acc + functools.reduce(lambda a, b: a + b, split(term))

        return lax.fori_loop(0, Z, one, jnp.zeros((levels, HD), F32))

    def second_pass(g, s):
        both = fin[g, s]
        prob = probs[g, s] * both[0:1]
        dscore = prob * (dprobs[g, s] - both[1:2])
        prob_b = prob.astype(BF16)
        dscore_b = dscore.astype(BF16)
        dq = lax.dot_general(kt[g], dscore_b, NN, preferred_element_type=F32)
        dq_all[g, s] = dq.T
        dv_acc[g] += lax.dot_general(prob_b, qo[s, g, 1], NN, preferred_element_type=F32)
        dk_acc[g] += lax.dot_general(dscore_b, qo[s, g, 0], NN, preferred_element_type=F32)

    def kv_finish(g):
        for which, acc in ((0, dk_acc), (1, dv_acc)):
            kv_grad(g, which).wait_recv()
            total = acc[g, 0:pre] + kv_in[g, which].astype(F32)
            if which == 0:
                total = total * SCALE
            kv_done[g, which] = total.astype(BF16)
            kv_store(g, which).start()

    def kv_store(g, which):
        hbm = (dk_hbm, dv_hbm)[which]
        return pltpu.make_async_copy(
            kv_done.at[g, which], hbm.at[0, :, pl.ds(g * HD, HD)], out_sem.at[g, which])

    def dq_store(g, j):
        return pltpu.make_async_copy(
            dq_done.at[g, pl.ds(j * cand, cand), :],
            dq_hbm.at[0, :, pl.ds((g * group + j) * HD, HD)],
            out_sem.at[g, 2 + j])

    def gather_tick(t, _):
        k, g = t // kv, t % kv

        for i in range(kv):
            @pl.when((k == 0) & (g == i))
            def _():
                for which in range(2):
                    kv_copy(i, which).wait()
                kt[i] = ks[i].astype(F32).T.astype(BF16)

        @pl.when((k >= 1) & (k < 4))
        def _():
            for part in range(2):
                for way in range(2):
                    gather(g, way, k, part).wait_recv()

                    @pl.when((k < 3) | (part == way))
                    def _():
                        gather(g, way, k + 1, part).start()

        @pl.when(k == 4)
        def _():
            gather(g, 0, 4, 0).wait_recv()
            gather(g, 1, 4, 1).wait_recv()

        def chunk(c, _):
            first_pass(g, jnp.where(c == 0, (Z - k) % Z, k))
            return 0

        lax.fori_loop(0, jnp.where((k == 0) | (k == 4), 1, 2), chunk, 0)

        @pl.when(k == 3)
        def _():
            for o in (5, 3, 6, 2, 7, 1):
                stat_a(g, o).start()

        @pl.when(k == 4)
        def _():
            for o in (5, 3, 6, 2, 7, 1):
                stat_a(g, o).wait()
            combine(g)
            st_all[g, 0, 1] = st_loc[g, 4]
            for o in (4, 5, 3, 6, 2, 7, 1):
                stat_b(g, o).start()

        return 0

    lax.fori_loop(0, 5 * kv, gather_tick, 0)

    def stats(g):
        for o in (1, 7, 2, 6, 3, 5, 4):
            stat_b(g, o).wait()
        term = finish(g)
        t_mid[0] = term if g == 0 else t_mid[0] + term
        if g == kv - 1:
            for i in range(len(t1_codes)):
                t1_copy(i).start()

    def scatter_first(g):
        for way in range(2):
            at = pl.ds(way * half, half)
            rs_out[g, way, 0, at, :] = dq_all[g, 4, at, :].astype(BF16)
            scatter(g, way, 0, way).start()

    def scatter_next(g, step):
        for part in range(2):
            for way in range(2):
                at = pl.ds(part * half, half)
                if step > 1 or part == way:
                    scatter(g, way, step - 1, part).wait_recv()
                s = 4 + step if way == 0 else 4 - step
                rs_out[g, way, step, at, :] = (
                    dq_all[g, s, at, :] + rs_in[g, way, step - 1, at, :].astype(F32)
                ).astype(BF16)
                scatter(g, way, step, part).start()

    def scatter_last(g):
        for part in range(2):
            at = pl.ds(part * half, half)
            for way in range(2):
                scatter(g, way, 3, part).wait_recv()
            dq = (dq_all[g, 0, at, :] + rs_in[g, 0, 3, at, :].astype(F32)
                  + rs_in[g, 1, 3, at, :].astype(F32))
            dq_done[g, at, :] = (dq * SCALE).astype(BF16)
        for j in range(group):
            dq_store(g, j).start()

    def kv_send_off(g):
        for which, acc in ((0, dk_acc), (1, dv_acc)):
            kv_out[g, which] = acc[g, pre:2 * pre].astype(BF16)
            kv_grad(g, which).start()

    order = [(0, 4), (0, 5), (0, 3), (0, 6), (0, 2), (1, 4), (0, 7), (0, 1), (1, 5), (1, 3),
             (0, 0), (1, 6), (1, 2), (1, 7), (1, 1), (1, 0)]
    before = {0: [lambda: stats(0)], 5: [lambda: stats(1)]}
    after = {
        0: [lambda: scatter_first(0)],
        5: [lambda: scatter_first(1), lambda: scatter_next(0, 1)],
        10: [lambda: kv_send_off(0)],
        11: [lambda: scatter_next(1, 1), lambda: scatter_next(0, 2)],
        15: [lambda: kv_send_off(1)],
    }

    def grad_tick(e, _):
        for at, calls in before.items():
            @pl.when(e == at)
            def _():
                for call in calls:
                    call()

        g = jnp.int32(0)
        s = jnp.int32(0)
        for i, (a, b) in enumerate(order):
            g = jnp.where(e == i, a, g)
            s = jnp.where(e == i, b, s)
        second_pass(g, s)

        for at, calls in after.items():
            @pl.when(e == at)
            def _():
                for call in calls:
                    call()
        return 0

    lax.fori_loop(0, len(order), grad_tick, 0)

    for i in range(len(t1_codes)):
        t1_copy(i).wait()
    t_mid[1] = t_mid[0] + sum(t_in1[i] for i in range(len(t1_codes)))
    for i in range(len(t2_codes)):
        t2_copy(i).start()

    scatter_next(1, 2)
    scatter_next(0, 3)
    kv_finish(0)
    scatter_next(1, 3)
    scatter_last(0)
    kv_finish(1)

    for g in range(kv):
        for way in range(2):
            for part in range(2):
                for step in range(1, 5):
                    if step < 4 or part == way:
                        gather(g, way, step, part).wait_send()
                for step in range(4):
                    if step > 0 or part == way:
                        scatter(g, way, step, part).wait_send()
        for which in range(2):
            kv_grad(g, which).wait_send()

    for i in range(len(t2_codes)):
        t2_copy(i).wait()
    total = t_mid[1] + sum(t_in2[i] for i in range(len(t2_codes)))
    total = jnp.sum(total, axis=1, keepdims=True)
    place = lax.broadcasted_iota(jnp.int32, (levels, levels), 0)
    across = lax.broadcasted_iota(jnp.int32, (levels, levels), 1)
    dt_ref[...] = jnp.sum(
        jnp.where(place == across, total, 0.0), axis=0, keepdims=True)

    scatter_last(1)
    for g in range(kv):
        for which in range(2):
            kv_store(g, which).wait()
        for j in range(group):
            dq_store(g, j).wait()


def shards(queries, keys, values, grad_out, counts, rate_table, rate_index):
    n_head, n_req = lax.axis_size("head"), lax.axis_size("req")
    cand, pre = queries.shape[1], keys.shape[1]
    kv = keys.shape[2] // HD
    group = queries.shape[2] // keys.shape[2]
    levels = rate_table.shape[0]
    rows = group * cand
    lanes = rows // HD
    first = Z * min(n_req, 2) - 1
    second = n_head * 2 * (n_req // min(n_req, 2)) - 1
    any_ = pl.BlockSpec(memory_space=pl.ANY)
    smem = pl.BlockSpec(memory_space=pltpu.SMEM)
    vmem = pl.BlockSpec(memory_space=pltpu.VMEM)
    dma = pltpu.SemaphoreType.DMA
    out = pl.pallas_call(
        functools.partial(kernel, n_head, n_req, cand, pre, group, kv, levels),
        out_shape=(
            jax.ShapeDtypeStruct(queries.shape, BF16),
            jax.ShapeDtypeStruct(keys.shape, BF16),
            jax.ShapeDtypeStruct(values.shape, BF16),
            jax.ShapeDtypeStruct((1, levels), F32),
        ),
        in_specs=[smem, smem, vmem, any_, any_, any_, any_],
        out_specs=(any_, any_, any_, vmem),
        scratch_shapes=[
            pltpu.VMEM((Z, kv, 2, rows, HD), BF16),
            pltpu.VMEM((kv, 2 * pre, HD), BF16),
            pltpu.VMEM((kv, 2 * pre, HD), BF16),
            pltpu.VMEM((kv, HD, 2 * pre), BF16),
            pltpu.VMEM((1, pre), jnp.int32),
            pltpu.VMEM((2 * pre, HD), F32),
            pltpu.VMEM((levels, 2 * pre), BF16),
            pltpu.VMEM((kv, Z, 2 * pre, rows), F32),
            pltpu.VMEM((kv, Z, 2 * pre, rows), F32),
            pltpu.VMEM((kv, Z, 1, rows), F32),
            pltpu.VMEM((kv, Z, 1, rows), F32),
            pltpu.VMEM((kv, Z, 2, rows), F32),
            pltpu.VMEM((kv, Z, levels, rows), F32),
            pltpu.VMEM((kv, Z, levels, rows), F32),
            pltpu.VMEM((kv, Z, 2 * lanes, HD), F32),
            pltpu.VMEM((kv, Z, 2 * lanes, HD), F32),
            pltpu.VMEM((kv, Z, 2, 2 * lanes, HD), F32),
            pltpu.VMEM((kv, Z, rows, HD), F32),
            pltpu.VMEM((kv, 2, 4, rows, HD), BF16),
            pltpu.VMEM((kv, 2, 4, rows, HD), BF16),
            pltpu.VMEM((kv, rows, HD), BF16),
            pltpu.VMEM((kv, 2 * pre, HD), F32),
            pltpu.VMEM((kv, 2 * pre, HD), F32),
            pltpu.VMEM((kv, 2, pre, HD), BF16),
            pltpu.VMEM((kv, 2, pre, HD), BF16),
            pltpu.VMEM((kv, 2, pre, HD), BF16),
            pltpu.VMEM((2, levels, HD), F32),
            pltpu.VMEM((first, levels, HD), F32),
            pltpu.VMEM((second, levels, HD), F32),
            dma((kv * (2 * group + 2),)),
            dma((kv, 2 + group)),
            dma((kv, 2)),
            dma((kv, 2)),
            dma,
            dma,
            dma((kv, 2, 2, 4)),
            dma((kv, 2, 2, 4)),
            dma((kv, Z)),
            dma((kv, Z)),
            dma((kv, Z)),
            dma((kv, Z)),
            dma((kv, 2, 4, 2)),
            dma((kv, 2, 4, 2)),
            dma((kv, 2)),
            dma((kv, 2)),
            dma((first,)),
            dma((first,)),
            dma((second,)),
            dma((second,)),
        ],
        compiler_params=pltpu.CompilerParams(
            collective_id=0, has_side_effects=True, vmem_limit_bytes=60 * 1024 * 1024),
    )(counts, rate_table, rate_index, queries, keys, values, grad_out)
    return out[0], out[1], out[2], out[3].reshape(levels)


def solution(mesh):
    split = P("req", "ctx", "head")
    return jax.shard_map(
        shards,
        mesh=mesh,
        in_specs=(split, split, split, split, P("req"), P(), P("req", "ctx")),
        out_specs=(split, split, split, P()),
        check_vma=False,
    )
```

```python
import functools

import jax
import jax.numpy as jnp
from jax import lax
from jax.experimental import pallas as pl
from jax.experimental.pallas import tpu as pltpu
from jax.sharding import PartitionSpec as P

HD = 128
Z = 8
SCALE = 128.0 ** (-0.5)
LOG2E = 1.4426950408889634
MESH = pl.DeviceIdType.MESH
F32 = jnp.float32
BF16 = jnp.bfloat16
NT = (((1,), (1,)), ((), ()))
TN = (((0,), (0,)), ((), ()))
NN = (((1,), (0,)), ((), ()))
NEAR = (6, 2, 7, 1)
FAR = (4, 5, 3)


def kernel(
    n_head, n_req, cand, pre, group, kv, levels,
    counts_ref, table_ref, index_ref, q_hbm, k_hbm, v_hbm, o_hbm,
    dq_hbm, dk_hbm, dv_hbm, dt_ref,
    qo, ks, vs, kt, idx_par, bias, onehot,
    probs, dprobs, peaks, deltas, fin, lev_a, lev_b, st_loc, st_in, st_all,
    dq_all, rs_out, rs_in, dq_done, dk_acc, dv_acc, kv_out, kv_in, kv_done,
    t_mid, t_in1, t_in2, t_in3,
    in_sem, out_sem, kv_send, kv_recv, ix_send, ix_recv,
    ag_send, ag_recv, sa_send, sa_recv, sb_send, sb_recv,
    rs_send, rs_recv, dk_send, dk_recv,
    t1_send, t1_recv, t2_send, t2_recv, t3_send, t3_recv,
):
    rows = group * cand
    half = rows // 2
    lanes = rows // HD
    n_core = min(n_req, 2)
    n_hi = n_req // n_core
    ctx = lax.axis_index("ctx")
    head = lax.axis_index("head")
    req = lax.axis_index("req")
    y = ctx // Z
    z = ctx % Z
    hi = req // n_core
    core = req % n_core

    def along_z(by):
        return {"ctx": y * Z + (z + by) % Z}

    partner = {"ctx": (1 - y) * Z + z}
    right, left = along_z(1), along_z(Z - 1)
    far_right, far_left = along_z(2), along_z(Z - 2)
    t2_codes = [(a, b) for a in range(n_head) for b in range(n_core)][1:]
    t3_codes = [(a, b) for a in range(2) for b in range(n_hi)][1:]

    def t2_peer(a, b):
        return {"head": (head + a) % n_head, "req": hi * n_core + (core + b) % n_core}

    def t3_peer(a, b):
        return {
            "ctx": ((y + a) % 2) * Z + z, "req": ((hi + b) % n_hi) * n_core + core}

    barrier = pltpu.get_barrier_semaphore()
    peers = [left, right]
    peers += [t2_peer(*code) for code in t2_codes] + [t3_peer(*code) for code in t3_codes]
    for peer in peers:
        pl.semaphore_signal(barrier, inc=1, device_id=peer, device_id_type=MESH)

    loads, late_loads = [], []
    for g in range(kv):
        for j in range(group):
            lo = (g * group + j) * HD
            for part, src in ((0, q_hbm), (1, o_hbm)):
                loads.append(pltpu.make_async_copy(
                    src.at[0, :, pl.ds(lo, HD)],
                    qo.at[0, g, part, pl.ds(j * cand, cand), :],
                    in_sem.at[len(loads)]))
    for g in range(kv):
        for src, dst in ((k_hbm, ks), (v_hbm, vs)):
            late_loads.append(pltpu.make_async_copy(
                src.at[0, :, pl.ds(g * HD, HD)],
                dst.at[g, pl.ds(0, pre), :],
                in_sem.at[len(loads) + len(late_loads)]))
    for copy in loads + late_loads:
        copy.start()

    dk_acc[...] = jnp.zeros_like(dk_acc)
    dv_acc[...] = jnp.zeros_like(dv_acc)

    level = lax.broadcasted_iota(jnp.int32, (levels, HD), 0)
    table = jnp.zeros((levels, HD), F32)
    for i in range(levels):
        table = jnp.where(level == i, table_ref[i], table)
    table = table.astype(BF16)

    def offsets(index, place):
        hot = (lax.broadcasted_iota(jnp.int32, (levels, pre), 0) == index)
        hot = hot.astype(F32).astype(BF16)
        onehot[:, pl.ds(place * pre, pre)] = hot
        bias[pl.ds(place * pre, pre), :] = lax.dot_general(
            hot, table, TN, preferred_element_type=F32) * LOG2E

    offsets(index_ref[...], 0)

    for copy in loads + late_loads:
        copy.wait()
    live = counts_ref[0] - ctx * cand
    slot = lax.rem(lax.broadcasted_iota(jnp.int32, (rows, HD), 0), cand)
    for g in range(kv):
        qo[0, g, 1] = jnp.where(slot < live, qo[0, g, 1], jnp.zeros((rows, HD), BF16))

    pl.semaphore_wait(barrier, len(peers))

    def remote(src, dst, send, recv, device):
        return pltpu.make_async_remote_copy(
            src_ref=src, dst_ref=dst, send_sem=send, recv_sem=recv,
            device_id=device, device_id_type=MESH)

    def gather(g, way, step, part):
        if way == 0:
            src, dst, device = lax.rem(9 - step, Z), Z - step, right
        else:
            src, dst, device = step - 1, step, left
        return remote(
            qo.at[src, g, part], qo.at[dst, g, part],
            ag_send.at[g, way, part, step - 1], ag_recv.at[g, way, part, step - 1], device)

    def kv_copy(g, which):
        ref = (ks, vs)[which]
        return remote(
            ref.at[g, pl.ds(0, pre), :], ref.at[g, pl.ds(pre, pre), :],
            kv_send.at[g, which], kv_recv.at[g, which], partner)

    ix_copy = remote(index_ref, idx_par, ix_send, ix_recv, partner)

    def stat_a(g, o):
        return remote(
            st_loc.at[g, o], st_in.at[g, o],
            sa_send.at[g, o], sa_recv.at[g, o], along_z(o))

    def stat_b(g, o):
        return remote(
            st_all.at[g, 0], st_all.at[g, o],
            sb_send.at[g, o], sb_recv.at[g, o], along_z(o))

    def scatter(g, way, step, part):
        at = pl.ds(part * half, half)
        return remote(
            rs_out.at[g, way, step, at, :], rs_in.at[g, way, step, at, :],
            rs_send.at[g, way, step, part], rs_recv.at[g, way, step, part],
            (far_left, far_right)[way] if step == 0 else (left, right)[way])

    def kv_grad(g, which):
        return remote(
            kv_out.at[g, which], kv_in.at[g, which],
            dk_send.at[g, which], dk_recv.at[g, which], partner)

    def t1_copy(o):
        return remote(
            t_mid.at[0], t_in1.at[o], t1_send.at[o], t1_recv.at[o], along_z(o))

    def t2_copy(i):
        return remote(
            t_mid.at[1], t_in2.at[i], t2_send.at[i], t2_recv.at[i], t2_peer(*t2_codes[i]))

    def t3_copy(i):
        return remote(
            t_mid.at[2], t_in3.at[i], t3_send.at[i], t3_recv.at[i], t3_peer(*t3_codes[i]))

    for g in range(kv):
        for part in range(2):
            for way in range(2):
                gather(g, way, 1, part).start()
        if g == 0:
            ix_copy.start()
        for which in range(2):
            kv_copy(g, which).start()

    def split(row):
        return [row[:, i * HD:(i + 1) * HD] for i in range(lanes)]

    def joined(block):
        return jnp.concatenate([block[i:i + 1] for i in range(lanes)], axis=1)

    def first_pass(g, s):
        q_blk = qo[s, g, 0]
        o_blk = qo[s, g, 1]
        off = jnp.concatenate([bias[...]] * lanes, axis=1)
        scores = lax.dot_general(ks[g], q_blk, NT, preferred_element_type=F32)
        scores = scores * (SCALE * LOG2E) + off
        peak = jnp.max(scores, axis=0, keepdims=True)
        prob = jnp.exp2(scores - peak)
        total = jnp.sum(prob, axis=0, keepdims=True)
        dprob = lax.dot_general(vs[g], o_blk, NT, preferred_element_type=F32)
        delta = jnp.sum(prob * dprob, axis=0, keepdims=True) / total
        probs[g, s] = prob
        dprobs[g, s] = dprob
        peaks[g, s] = peak
        deltas[g, s] = delta
        lev_a[g, s] = lax.dot_general(
            onehot[...], (prob * (dprob - delta)).astype(BF16), NN,
            preferred_element_type=F32)
        lev_b[g, s] = lax.dot_general(
            onehot[...], prob.astype(BF16), NN, preferred_element_type=F32)
        lse = peak + jnp.log2(total)
        st_loc[g, s] = jnp.concatenate(split(lse) + split(delta), axis=0)

    def merged(parts):
        lse = [p[0:lanes] for p in parts]
        top = functools.reduce(jnp.maximum, lse)
        total = top + jnp.log2(sum(jnp.exp2(v - top) for v in lse))
        delta = sum(jnp.exp2(v - total) * p[lanes:] for v, p in zip(lse, parts))
        return total, delta

    def combine(g):
        total, delta = merged([st_loc[g, 0]] + [st_in[g, o] for o in NEAR])
        st_all[g, 0, 0] = jnp.concatenate([total, delta], axis=0)

    def finish(g):
        def one(s, acc):
            total, delta = merged([st_all[g, lax.rem(Z - s, Z), 0]] + [
                st_all[g, lax.rem(Z + o - s, Z), 1 + i] for i, o in enumerate(FAR)])
            delta = joined(delta)
            factor = jnp.exp2(peaks[g, s] - joined(total))
            fin[g, s] = jnp.concatenate([factor, delta], axis=0)
            term = factor * (lev_a[g, s] - (delta - deltas[g, s]) * lev_b[g, s])
            return acc + functools.reduce(lambda a, b: a + b, split(term))

        return lax.fori_loop(0, Z, one, jnp.zeros((levels, HD), F32))

    def second_pass(g, s):
        both = fin[g, s]
        prob = probs[g, s] * both[0:1]
        dscore = prob * (dprobs[g, s] - both[1:2])
        prob_b = prob.astype(BF16)
        dscore_b = dscore.astype(BF16)
        dq = lax.dot_general(kt[g], dscore_b, NN, preferred_element_type=F32)
        dq_all[g, s] = dq.T
        dv_acc[g] += lax.dot_general(prob_b, qo[s, g, 1], NN, preferred_element_type=F32)
        dk_acc[g] += lax.dot_general(dscore_b, qo[s, g, 0], NN, preferred_element_type=F32)

    def kv_finish(g):
        for which, acc in ((0, dk_acc), (1, dv_acc)):
            kv_grad(g, which).wait_recv()
            total = acc[g, 0:pre] + kv_in[g, which].astype(F32)
            if which == 0:
                total = total * SCALE
            kv_done[g, which] = total.astype(BF16)
            kv_store(g, which).start()

    def kv_store(g, which):
        hbm = (dk_hbm, dv_hbm)[which]
        return pltpu.make_async_copy(
            kv_done.at[g, which], hbm.at[0, :, pl.ds(g * HD, HD)], out_sem.at[g, which])

    def dq_store(g, j):
        return pltpu.make_async_copy(
            dq_done.at[g, pl.ds(j * cand, cand), :],
            dq_hbm.at[0, :, pl.ds((g * group + j) * HD, HD)],
            out_sem.at[g, 2 + j])

    def gather_tick(t, _):
        k, g = 1 + t // kv, t % kv

        @pl.when(k < 4)
        def _():
            for part in range(2):
                for way in range(2):
                    gather(g, way, k, part).wait_recv()

                    @pl.when((k < 3) | (part == way))
                    def _():
                        gather(g, way, k + 1, part).start()

        @pl.when(k == 4)
        def _():
            for o in NEAR:
                stat_a(g, o).wait()
            combine(g)
            gather(g, 0, 4, 0).wait_recv()
            gather(g, 1, 4, 1).wait_recv()

        for i in range(kv):
            @pl.when((k == 1) & (g == i))
            def _():
                if i == 0:
                    ix_copy.wait()
                    offsets(idx_par[...], 1)
                for which in range(2):
                    kv_copy(i, which).wait()
                kt[i] = ks[i].astype(F32).T.astype(BF16)

        def chunk(c, _):
            first_pass(g, jnp.where(c == 0, Z - k, jnp.where(c == 1, k, 0)))
            return 0

        lax.fori_loop(0, jnp.where(k == 4, 1, jnp.where(k == 1, 3, 2)), chunk, 0)

        @pl.when(k == 2)
        def _():
            for o in NEAR:
                stat_a(g, o).start()

        @pl.when(k == 4)
        def _():
            for i, o in enumerate(FAR):
                st_all[g, 0, 1 + i] = st_loc[g, o]
            for o in (4, 5, 3, 6, 2, 7, 1):
                stat_b(g, o).start()

        return 0

    lax.fori_loop(0, 4 * kv, gather_tick, 0)

    def stats(g):
        for o in (1, 7, 2, 6, 3, 5, 4):
            stat_b(g, o).wait()
        term = finish(g)
        place = lax.broadcasted_iota(jnp.int32, (levels, HD), 0)
        across = lax.broadcasted_iota(jnp.int32, (levels, HD), 1)
        term = jnp.sum(term, axis=1, keepdims=True)
        term = jnp.sum(jnp.where(place == across, term, 0.0), axis=0, keepdims=True)
        t_mid[0] = term if g == 0 else t_mid[0] + term

    def table_first():
        for o in range(1, Z):
            t1_copy(o).start()

    def table_second():
        for o in range(1, Z):
            t1_copy(o).wait()
        t_mid[1] = t_mid[0] + sum(t_in1[o] for o in range(1, Z))
        for i in range(len(t2_codes)):
            t2_copy(i).start()

    def table_third():
        for i in range(len(t2_codes)):
            t2_copy(i).wait()
        t_mid[2] = t_mid[1] + sum(t_in2[i] for i in range(len(t2_codes)))
        for i in range(len(t3_codes)):
            t3_copy(i).start()

    def scatter_first(g):
        for way in range(2):
            at = pl.ds(way * half, half)
            rs_out[g, way, 0, at, :] = dq_all[g, 4, at, :].astype(BF16)
            scatter(g, way, 0, way).start()

    def scatter_next(g, step):
        for part in range(2):
            for way in range(2):
                at = pl.ds(part * half, half)
                dq = dq_all[g, 4 + step if way == 0 else 4 - step, at, :]
                if step == 2 and part == way:
                    scatter(g, way, 0, part).wait_recv()
                    dq = dq + rs_in[g, way, 0, at, :].astype(F32)
                if step > 1:
                    scatter(g, way, step - 1, part).wait_recv()
                    dq = dq + rs_in[g, way, step - 1, at, :].astype(F32)
                rs_out[g, way, step, at, :] = dq.astype(BF16)
                scatter(g, way, step, part).start()

    def scatter_last(g):
        for part in range(2):
            at = pl.ds(part * half, half)
            for way in range(2):
                scatter(g, way, 3, part).wait_recv()
            dq = (dq_all[g, 0, at, :] + rs_in[g, 0, 3, at, :].astype(F32)
                  + rs_in[g, 1, 3, at, :].astype(F32))
            dq_done[g, at, :] = (dq * SCALE).astype(BF16)
        for j in range(group):
            dq_store(g, j).start()

    def kv_send_off(g):
        for which, acc in ((0, dk_acc), (1, dv_acc)):
            kv_out[g, which] = acc[g, pre:2 * pre].astype(BF16)
            kv_grad(g, which).start()

    order = [(0, 4), (0, 5), (0, 3), (1, 4), (1, 5), (1, 3), (0, 6), (0, 2), (1, 6), (1, 2),
             (0, 7), (0, 1), (0, 0), (1, 7), (1, 1), (1, 0)]
    before = {0: [lambda: stats(0)], 3: [lambda: stats(1), table_first]}
    after = {
        0: [lambda: scatter_first(0)],
        2: [lambda: scatter_next(0, 1)],
        3: [lambda: scatter_first(1)],
        5: [lambda: scatter_next(1, 1)],
        9: [lambda: scatter_next(0, 2), table_second],
        12: [lambda: scatter_next(1, 2), lambda: kv_send_off(0)],
        15: [lambda: kv_send_off(1), table_third],
    }

    def grad_tick(e, _):
        for at, calls in before.items():
            @pl.when(e == at)
            def _():
                for call in calls:
                    call()

        g = jnp.int32(0)
        s = jnp.int32(0)
        for i, (a, b) in enumerate(order):
            g = jnp.where(e == i, a, g)
            s = jnp.where(e == i, b, s)
        second_pass(g, s)

        for at, calls in after.items():
            @pl.when(e == at)
            def _():
                for call in calls:
                    call()
        return 0

    lax.fori_loop(0, len(order), grad_tick, 0)

    scatter_next(0, 3)
    scatter_next(1, 3)
    kv_finish(0)
    scatter_last(0)

    for g in range(kv):
        for way in range(2):
            for part in range(2):
                for step in range(1, 5):
                    if step < 4 or part == way:
                        gather(g, way, step, part).wait_send()
                for step in range(4):
                    if step > 0 or part == way:
                        scatter(g, way, step, part).wait_send()
        for which in range(2):
            kv_grad(g, which).wait_send()

    kv_finish(1)
    scatter_last(1)
    for i in range(len(t3_codes)):
        t3_copy(i).wait()
    total = t_mid[2] + sum(t_in3[i] for i in range(len(t3_codes)))
    dt_ref[...] = total[:, 0:levels]

    for g in range(kv):
        for which in range(2):
            kv_store(g, which).wait()
        for j in range(group):
            dq_store(g, j).wait()


def placed(*refs):
    sources, results, stages, sem = refs[:4], refs[4:8], refs[8:12], refs[12]
    fetch = [pltpu.make_async_copy(a, b, sem.at[0, i])
             for i, (a, b) in enumerate(zip(sources, stages))]
    store = [pltpu.make_async_copy(a, b, sem.at[1, i])
             for i, (a, b) in enumerate(zip(stages, results))]
    for copy in fetch:
        copy.start()
    for first, second in zip(fetch, store):
        first.wait()
        second.start()
    for copy in store:
        copy.wait()


def shards(queries, keys, values, grad_out, counts, rate_table, rate_index):
    n_head, n_req = lax.axis_size("head"), lax.axis_size("req")
    cand, pre = queries.shape[1], keys.shape[1]
    kv = keys.shape[2] // HD
    group = queries.shape[2] // keys.shape[2]
    levels = rate_table.shape[0]
    rows = group * cand
    lanes = rows // HD
    second = max(n_head * min(n_req, 2) - 1, 1)
    third = 2 * (n_req // min(n_req, 2)) - 1
    any_ = pl.BlockSpec(memory_space=pl.ANY)
    smem = pl.BlockSpec(memory_space=pltpu.SMEM)
    vmem = pl.BlockSpec(memory_space=pltpu.VMEM)
    dma = pltpu.SemaphoreType.DMA
    out = pl.pallas_call(
        functools.partial(kernel, n_head, n_req, cand, pre, group, kv, levels),
        out_shape=(
            jax.ShapeDtypeStruct(queries.shape, BF16),
            jax.ShapeDtypeStruct(keys.shape, BF16),
            jax.ShapeDtypeStruct(values.shape, BF16),
            jax.ShapeDtypeStruct((1, levels), F32),
        ),
        in_specs=[smem, smem, vmem, any_, any_, any_, any_],
        out_specs=(any_, any_, any_, vmem),
        scratch_shapes=[
            pltpu.VMEM((Z, kv, 2, rows, HD), BF16),
            pltpu.VMEM((kv, 2 * pre, HD), BF16),
            pltpu.VMEM((kv, 2 * pre, HD), BF16),
            pltpu.VMEM((kv, HD, 2 * pre), BF16),
            pltpu.VMEM((1, pre), jnp.int32),
            pltpu.VMEM((2 * pre, HD), F32),
            pltpu.VMEM((levels, 2 * pre), BF16),
            pltpu.VMEM((kv, Z, 2 * pre, rows), F32),
            pltpu.VMEM((kv, Z, 2 * pre, rows), F32),
            pltpu.VMEM((kv, Z, 1, rows), F32),
            pltpu.VMEM((kv, Z, 1, rows), F32),
            pltpu.VMEM((kv, Z, 2, rows), F32),
            pltpu.VMEM((kv, Z, levels, rows), F32),
            pltpu.VMEM((kv, Z, levels, rows), F32),
            pltpu.VMEM((kv, Z, 2 * lanes, HD), F32),
            pltpu.VMEM((kv, Z, 2 * lanes, HD), F32),
            pltpu.VMEM((kv, Z, 4, 2 * lanes, HD), F32),
            pltpu.VMEM((kv, Z, rows, HD), F32),
            pltpu.VMEM((kv, 2, 4, rows, HD), BF16),
            pltpu.VMEM((kv, 2, 4, rows, HD), BF16),
            pltpu.VMEM((kv, rows, HD), BF16),
            pltpu.VMEM((kv, 2 * pre, HD), F32),
            pltpu.VMEM((kv, 2 * pre, HD), F32),
            pltpu.VMEM((kv, 2, pre, HD), BF16),
            pltpu.VMEM((kv, 2, pre, HD), BF16),
            pltpu.VMEM((kv, 2, pre, HD), BF16),
            pltpu.VMEM((3, 1, HD), F32),
            pltpu.VMEM((Z, 1, HD), F32),
            pltpu.VMEM((second, 1, HD), F32),
            pltpu.VMEM((third, 1, HD), F32),
            dma((kv * (2 * group + 2),)),
            dma((kv, 2 + group)),
            dma((kv, 2)),
            dma((kv, 2)),
            dma,
            dma,
            dma((kv, 2, 2, 4)),
            dma((kv, 2, 2, 4)),
            dma((kv, Z)),
            dma((kv, Z)),
            dma((kv, Z)),
            dma((kv, Z)),
            dma((kv, 2, 4, 2)),
            dma((kv, 2, 4, 2)),
            dma((kv, 2)),
            dma((kv, 2)),
            dma((Z,)),
            dma((Z,)),
            dma((second,)),
            dma((second,)),
            dma((third,)),
            dma((third,)),
        ],
        compiler_params=pltpu.CompilerParams(
            collective_id=0, has_side_effects=True, vmem_limit_bytes=60 * 1024 * 1024),
    )(counts, rate_table, rate_index, queries, keys, values, grad_out)
    out = pl.pallas_call(
        placed,
        out_shape=tuple(jax.ShapeDtypeStruct(x.shape, x.dtype) for x in out),
        in_specs=[any_] * 4,
        out_specs=(any_,) * 4,
        scratch_shapes=[pltpu.VMEM(x.shape, x.dtype) for x in out] + [dma((2, 4))],
        compiler_params=pltpu.CompilerParams(vmem_limit_bytes=60 * 1024 * 1024),
    )(*out)
    return out[0], out[1], out[2], out[3].reshape(levels)


def solution(mesh):
    split = P("req", "ctx", "head")
    return jax.shard_map(
        shards,
        mesh=mesh,
        in_specs=(split, split, split, split, P("req"), P(), P("req", "ctx")),
        out_specs=(split, split, split, P()),
        check_vma=False,
    )
```

```python
import functools

import jax
import jax.numpy as jnp
from jax import lax
from jax.experimental import pallas as pl
from jax.experimental.pallas import tpu as pltpu
from jax.sharding import PartitionSpec as P

HD = 128
Z = 8
SCALE = 128.0 ** (-0.5)
LOG2E = 1.4426950408889634
MESH = pl.DeviceIdType.MESH
F32 = jnp.float32
BF16 = jnp.bfloat16
NT = (((1,), (1,)), ((), ()))
TN = (((0,), (0,)), ((), ()))
NN = (((1,), (0,)), ((), ()))
NEAR = (6, 2, 7, 1)
FAR = (4, 5, 3)
SHORT = (0, 1)


def kernel(
    n_head, n_req, cand, pre, group, kv, levels,
    counts_ref, table_ref, index_ref, q_hbm, k_hbm, v_hbm, o_hbm,
    dq_hbm, dk_hbm, dv_hbm, dt_ref,
    qo, ks, vs, kt, idx_par, bias, onehot,
    probs, dprobs, peaks, deltas, fin, lev_a, lev_b, st_loc, st_in, st_all,
    dq_all, rs_out, rs_in, dq_done, dk_acc, dv_acc, kv_out, kv_in, kv_done,
    t_mid, t_in1, t_in2, t_in3,
    in_sem, out_sem, kv_send, kv_recv, ix_send, ix_recv,
    ag_send, ag_recv, sa_send, sa_recv, sb_send, sb_recv,
    rs_send, rs_recv, dk_send, dk_recv,
    t1_send, t1_recv, t2_send, t2_recv, t3_send, t3_recv,
):
    rows = group * cand
    half = rows // 2
    lanes = rows // HD
    n_core = min(n_req, 2)
    n_hi = n_req // n_core
    ctx = lax.axis_index("ctx")
    head = lax.axis_index("head")
    req = lax.axis_index("req")
    y = ctx // Z
    z = ctx % Z
    hi = req // n_core
    core = req % n_core

    def along_z(by):
        return {"ctx": y * Z + (z + by) % Z}

    partner = {"ctx": (1 - y) * Z + z}
    right, left = along_z(1), along_z(Z - 1)
    far_right, far_left = along_z(2), along_z(Z - 2)
    t2_codes = [(a, b) for a in range(n_head) for b in range(n_core)][1:]
    t3_codes = [(a, b) for a in range(2) for b in range(n_hi)][1:]

    def t2_peer(a, b):
        return {"head": (head + a) % n_head, "req": hi * n_core + (core + b) % n_core}

    def t3_peer(a, b):
        return {
            "ctx": ((y + a) % 2) * Z + z, "req": ((hi + b) % n_hi) * n_core + core}

    barrier = pltpu.get_barrier_semaphore()
    peers = [left, right]
    peers += [t2_peer(*code) for code in t2_codes] + [t3_peer(*code) for code in t3_codes]
    for peer in peers:
        pl.semaphore_signal(barrier, inc=1, device_id=peer, device_id_type=MESH)

    loads, late_loads = [], []
    for g in range(kv):
        for j in range(group):
            lo = (g * group + j) * HD
            for part, src in ((0, q_hbm), (1, o_hbm)):
                loads.append(pltpu.make_async_copy(
                    src.at[0, :, pl.ds(lo, HD)],
                    qo.at[0, g, part, pl.ds(j * cand, cand), :],
                    in_sem.at[len(loads)]))
    for g in range(kv):
        for src, dst in ((k_hbm, ks), (v_hbm, vs)):
            late_loads.append(pltpu.make_async_copy(
                src.at[0, :, pl.ds(g * HD, HD)],
                dst.at[g, pl.ds(0, pre), :],
                in_sem.at[len(loads) + len(late_loads)]))
    for copy in loads + late_loads:
        copy.start()

    dk_acc[...] = jnp.zeros_like(dk_acc)
    dv_acc[...] = jnp.zeros_like(dv_acc)

    level = lax.broadcasted_iota(jnp.int32, (levels, HD), 0)
    table = jnp.zeros((levels, HD), F32)
    for i in range(levels):
        table = jnp.where(level == i, table_ref[i], table)
    table = table.astype(BF16)

    def offsets(index, place):
        hot = (lax.broadcasted_iota(jnp.int32, (levels, pre), 0) == index)
        hot = hot.astype(F32).astype(BF16)
        onehot[:, pl.ds(place * pre, pre)] = hot
        bias[pl.ds(place * pre, pre), :] = lax.dot_general(
            hot, table, TN, preferred_element_type=F32) * LOG2E

    offsets(index_ref[...], 0)

    for copy in loads + late_loads:
        copy.wait()
    live = counts_ref[0] - ctx * cand
    slot = lax.rem(lax.broadcasted_iota(jnp.int32, (rows, HD), 0), cand)
    for g in range(kv):
        qo[0, g, 1] = jnp.where(slot < live, qo[0, g, 1], jnp.zeros((rows, HD), BF16))

    pl.semaphore_wait(barrier, len(peers))

    def remote(src, dst, send, recv, device):
        return pltpu.make_async_remote_copy(
            src_ref=src, dst_ref=dst, send_sem=send, recv_sem=recv,
            device_id=device, device_id_type=MESH)

    def gather(g, way, step, part):
        if way == 0:
            src, dst, device = lax.rem(9 - step, Z), Z - step, right
        else:
            src, dst, device = step - 1, step, left
        return remote(
            qo.at[src, g, part], qo.at[dst, g, part],
            ag_send.at[g, way, part, step - 1], ag_recv.at[g, way, part, step - 1], device)

    def kv_copy(g, which):
        ref = (ks, vs)[which]
        return remote(
            ref.at[g, pl.ds(0, pre), :], ref.at[g, pl.ds(pre, pre), :],
            kv_send.at[g, which], kv_recv.at[g, which], partner)

    ix_copy = remote(index_ref, idx_par, ix_send, ix_recv, partner)

    def stat_a(g, o):
        return remote(
            st_loc.at[g, o], st_in.at[g, o],
            sa_send.at[g, o], sa_recv.at[g, o], along_z(o))

    def stat_b(g, o):
        return remote(
            st_all.at[g, 0], st_all.at[g, o],
            sb_send.at[g, o], sb_recv.at[g, o], along_z(o))

    def scatter(g, way, step, part):
        at = pl.ds(part * half, half)
        return remote(
            rs_out.at[g, way, step, at, :], rs_in.at[g, way, step, at, :],
            rs_send.at[g, way, step, part], rs_recv.at[g, way, step, part],
            (far_left, far_right)[way] if step == 0 and g in SHORT else (left, right)[way])

    def kv_grad(g, which):
        return remote(
            kv_out.at[g, which], kv_in.at[g, which],
            dk_send.at[g, which], dk_recv.at[g, which], partner)

    def t1_copy(o):
        return remote(
            t_mid.at[0], t_in1.at[o], t1_send.at[o], t1_recv.at[o], along_z(o))

    def t2_copy(i):
        return remote(
            t_mid.at[1], t_in2.at[i], t2_send.at[i], t2_recv.at[i], t2_peer(*t2_codes[i]))

    def t3_copy(i):
        return remote(
            t_mid.at[2], t_in3.at[i], t3_send.at[i], t3_recv.at[i], t3_peer(*t3_codes[i]))

    for g in range(kv):
        for part in range(2):
            for way in range(2):
                gather(g, way, 1, part).start()
        if g == 0:
            ix_copy.start()
        for which in range(2):
            kv_copy(g, which).start()

    def split(row):
        return [row[:, i * HD:(i + 1) * HD] for i in range(lanes)]

    def joined(block):
        return jnp.concatenate([block[i:i + 1] for i in range(lanes)], axis=1)

    def first_pass(g, s):
        q_blk = qo[s, g, 0]
        o_blk = qo[s, g, 1]
        off = jnp.concatenate([bias[...]] * lanes, axis=1)
        scores = lax.dot_general(ks[g], q_blk, NT, preferred_element_type=F32)
        scores = scores * (SCALE * LOG2E) + off
        peak = jnp.max(scores, axis=0, keepdims=True)
        prob = jnp.exp2(scores - peak)
        total = jnp.sum(prob, axis=0, keepdims=True)
        dprob = lax.dot_general(vs[g], o_blk, NT, preferred_element_type=F32)
        delta = jnp.sum(prob * dprob, axis=0, keepdims=True) / total
        probs[g, s] = prob
        dprobs[g, s] = dprob
        peaks[g, s] = peak
        deltas[g, s] = delta
        lev_a[g, s] = lax.dot_general(
            onehot[...], (prob * (dprob - delta)).astype(BF16), NN,
            preferred_element_type=F32)
        lev_b[g, s] = lax.dot_general(
            onehot[...], prob.astype(BF16), NN, preferred_element_type=F32)
        lse = peak + jnp.log2(total)
        st_loc[g, s] = jnp.concatenate(split(lse) + split(delta), axis=0)

    def merged(parts):
        lse = [p[0:lanes] for p in parts]
        top = functools.reduce(jnp.maximum, lse)
        total = top + jnp.log2(sum(jnp.exp2(v - top) for v in lse))
        delta = sum(jnp.exp2(v - total) * p[lanes:] for v, p in zip(lse, parts))
        return total, delta

    def combine(g):
        total, delta = merged([st_loc[g, 0]] + [st_in[g, o] for o in NEAR])
        st_all[g, 0, 0] = jnp.concatenate([total, delta], axis=0)

    def finish(g):
        acc = []
        for s in range(Z):
            total, delta = merged([st_all[g, (Z - s) % Z, 0]] + [
                st_all[g, (Z + o - s) % Z, 1 + i] for i, o in enumerate(FAR)])
            delta = joined(delta)
            factor = jnp.exp2(peaks[g, s] - joined(total))
            fin[g, s] = jnp.concatenate([factor, delta], axis=0)
            term = factor * (lev_a[g, s] - (delta - deltas[g, s]) * lev_b[g, s])
            acc += split(term)
        return sum(acc)

    def second_pass(g, s):
        both = fin[g, s]
        prob = probs[g, s] * both[0:1]
        dscore = prob * (dprobs[g, s] - both[1:2])
        prob_b = prob.astype(BF16)
        dscore_b = dscore.astype(BF16)
        dq = lax.dot_general(kt[g], dscore_b, NN, preferred_element_type=F32)
        dq_all[g, s] = dq.T
        dv_acc[g] += lax.dot_general(prob_b, qo[s, g, 1], NN, preferred_element_type=F32)
        dk_acc[g] += lax.dot_general(dscore_b, qo[s, g, 0], NN, preferred_element_type=F32)

    def kv_finish(g):
        for which, acc in ((0, dk_acc), (1, dv_acc)):
            kv_grad(g, which).wait_recv()
            total = acc[g, 0:pre] + kv_in[g, which].astype(F32)
            if which == 0:
                total = total * SCALE
            kv_done[g, which] = total.astype(BF16)
            kv_store(g, which).start()

    def kv_store(g, which):
        hbm = (dk_hbm, dv_hbm)[which]
        return pltpu.make_async_copy(
            kv_done.at[g, which], hbm.at[0, :, pl.ds(g * HD, HD)], out_sem.at[g, which])

    def dq_store(g, j):
        return pltpu.make_async_copy(
            dq_done.at[g, pl.ds(j * cand, cand), :],
            dq_hbm.at[0, :, pl.ds((g * group + j) * HD, HD)],
            out_sem.at[g, 2 + j])

    def gather_tick(t, _):
        k, g = 1 + t // kv, t % kv

        @pl.when(k < 4)
        def _():
            for part in range(2):
                for way in range(2):
                    gather(g, way, k, part).wait_recv()

                    @pl.when((k < 3) | (part == way))
                    def _():
                        gather(g, way, k + 1, part).start()

        @pl.when(k == 4)
        def _():
            for o in NEAR:
                stat_a(g, o).wait()
            combine(g)
            gather(g, 0, 4, 0).wait_recv()
            gather(g, 1, 4, 1).wait_recv()

        for i in range(kv):
            @pl.when((k == 1) & (g == i))
            def _():
                if i == 0:
                    ix_copy.wait()
                    offsets(idx_par[...], 1)
                for which in range(2):
                    kv_copy(i, which).wait()
                kt[i] = ks[i].astype(F32).T.astype(BF16)

        def chunk(c, _):
            first_pass(g, jnp.where(c == 0, Z - k, jnp.where(c == 1, k, 0)))
            return 0

        lax.fori_loop(0, jnp.where(k == 4, 1, jnp.where(k == 1, 3, 2)), chunk, 0)

        @pl.when(k == 2)
        def _():
            for o in NEAR:
                stat_a(g, o).start()

        @pl.when(k == 4)
        def _():
            for i, o in enumerate(FAR):
                st_all[g, 0, 1 + i] = st_loc[g, o]
            for o in (4, 5, 3, 6, 2, 7, 1):
                stat_b(g, o).start()

        return 0

    lax.fori_loop(0, 4 * kv, gather_tick, 0)

    def stats(g):
        for o in (1, 7, 2, 6, 3, 5, 4):
            stat_b(g, o).wait()
        term = finish(g)
        place = lax.broadcasted_iota(jnp.int32, (levels, HD), 0)
        across = lax.broadcasted_iota(jnp.int32, (levels, HD), 1)
        term = jnp.sum(term, axis=1, keepdims=True)
        term = jnp.sum(jnp.where(place == across, term, 0.0), axis=0, keepdims=True)
        t_mid[0] = term if g == 0 else t_mid[0] + term

    def table_first():
        for o in range(1, Z):
            t1_copy(o).start()

    def table_second():
        for o in range(1, Z):
            t1_copy(o).wait()
        t_mid[1] = t_mid[0] + sum(t_in1[o] for o in range(1, Z))
        for i in range(len(t2_codes)):
            t2_copy(i).start()

    def table_third():
        for i in range(len(t2_codes)):
            t2_copy(i).wait()
        t_mid[2] = t_mid[1] + sum(t_in2[i] for i in range(len(t2_codes)))
        for i in range(len(t3_codes)):
            t3_copy(i).start()

    def scatter_first(g):
        for way in range(2):
            at = pl.ds(way * half, half)
            rs_out[g, way, 0, at, :] = dq_all[g, 4, at, :].astype(BF16)
            scatter(g, way, 0, way).start()

    def scatter_next(g, step):
        for part in range(2):
            for way in range(2):
                at = pl.ds(part * half, half)
                dq = dq_all[g, 4 + step if way == 0 else 4 - step, at, :]
                if step == (2 if g in SHORT else 1) and part == way:
                    scatter(g, way, 0, part).wait_recv()
                    dq = dq + rs_in[g, way, 0, at, :].astype(F32)
                if step > 1:
                    scatter(g, way, step - 1, part).wait_recv()
                    dq = dq + rs_in[g, way, step - 1, at, :].astype(F32)
                rs_out[g, way, step, at, :] = dq.astype(BF16)
                scatter(g, way, step, part).start()

    def scatter_last(g):
        for part in range(2):
            at = pl.ds(part * half, half)
            for way in range(2):
                scatter(g, way, 3, part).wait_recv()
            dq = (dq_all[g, 0, at, :] + rs_in[g, 0, 3, at, :].astype(F32)
                  + rs_in[g, 1, 3, at, :].astype(F32))
            dq_done[g, at, :] = (dq * SCALE).astype(BF16)
        for j in range(group):
            dq_store(g, j).start()

    def kv_send_off(g):
        for which, acc in ((0, dk_acc), (1, dv_acc)):
            kv_out[g, which] = acc[g, pre:2 * pre].astype(BF16)
            kv_grad(g, which).start()

    order = [(0, 4), (0, 5), (0, 3), (1, 4), (1, 5), (1, 3), (0, 6), (0, 2), (1, 6), (1, 2),
             (0, 7), (0, 1), (0, 0), (1, 7), (1, 1), (1, 0)]
    before = {0: [lambda: stats(0)], 3: [lambda: stats(1), table_first]}
    after = {
        0: [lambda: scatter_first(0)],
        2: [lambda: scatter_next(0, 1)],
        3: [lambda: scatter_first(1)],
        5: [lambda: scatter_next(1, 1)],
        11: [lambda: scatter_next(0, 2)],
        12: [lambda: kv_send_off(0)],
        14: [lambda: scatter_next(1, 2), table_second],
        15: [lambda: kv_send_off(1)],
    }

    def grad_tick(e, _):
        for at, calls in before.items():
            @pl.when(e == at)
            def _():
                for call in calls:
                    call()

        g = jnp.int32(0)
        s = jnp.int32(0)
        for i, (a, b) in enumerate(order):
            g = jnp.where(e == i, a, g)
            s = jnp.where(e == i, b, s)
        second_pass(g, s)

        for at, calls in after.items():
            @pl.when(e == at)
            def _():
                for call in calls:
                    call()
        return 0

    lax.fori_loop(0, len(order), grad_tick, 0)

    scatter_next(0, 3)
    scatter_next(1, 3)
    table_third()
    kv_finish(0)
    scatter_last(0)

    for g in range(kv):
        for way in range(2):
            for part in range(2):
                for step in range(1, 5):
                    if step < 4 or part == way:
                        gather(g, way, step, part).wait_send()
                for step in range(4):
                    if step > 0 or part == way:
                        scatter(g, way, step, part).wait_send()
        for which in range(2):
            kv_grad(g, which).wait_send()

    kv_finish(1)
    scatter_last(1)
    for i in range(len(t3_codes)):
        t3_copy(i).wait()
    total = t_mid[2] + sum(t_in3[i] for i in range(len(t3_codes)))
    dt_ref[...] = total[:, 0:levels]

    for g in range(kv):
        for which in range(2):
            kv_store(g, which).wait()
        for j in range(group):
            dq_store(g, j).wait()


def placed(*refs):
    sources, results, stages, sem = refs[:4], refs[4:8], refs[8:12], refs[12]
    fetch = [pltpu.make_async_copy(a, b, sem.at[0, i])
             for i, (a, b) in enumerate(zip(sources, stages))]
    store = [pltpu.make_async_copy(a, b, sem.at[1, i])
             for i, (a, b) in enumerate(zip(stages, results))]
    for copy in fetch:
        copy.start()
    for first, second in zip(fetch, store):
        first.wait()
        second.start()
    for copy in store:
        copy.wait()


def shards(queries, keys, values, grad_out, counts, rate_table, rate_index):
    n_head, n_req = lax.axis_size("head"), lax.axis_size("req")
    cand, pre = queries.shape[1], keys.shape[1]
    kv = keys.shape[2] // HD
    group = queries.shape[2] // keys.shape[2]
    levels = rate_table.shape[0]
    rows = group * cand
    lanes = rows // HD
    second = max(n_head * min(n_req, 2) - 1, 1)
    third = 2 * (n_req // min(n_req, 2)) - 1
    any_ = pl.BlockSpec(memory_space=pl.ANY)
    smem = pl.BlockSpec(memory_space=pltpu.SMEM)
    vmem = pl.BlockSpec(memory_space=pltpu.VMEM)
    dma = pltpu.SemaphoreType.DMA
    out = pl.pallas_call(
        functools.partial(kernel, n_head, n_req, cand, pre, group, kv, levels),
        out_shape=(
            jax.ShapeDtypeStruct(queries.shape, BF16),
            jax.ShapeDtypeStruct(keys.shape, BF16),
            jax.ShapeDtypeStruct(values.shape, BF16),
            jax.ShapeDtypeStruct((1, levels), F32),
        ),
        in_specs=[smem, smem, vmem, any_, any_, any_, any_],
        out_specs=(any_, any_, any_, vmem),
        scratch_shapes=[
            pltpu.VMEM((Z, kv, 2, rows, HD), BF16),
            pltpu.VMEM((kv, 2 * pre, HD), BF16),
            pltpu.VMEM((kv, 2 * pre, HD), BF16),
            pltpu.VMEM((kv, HD, 2 * pre), BF16),
            pltpu.VMEM((1, pre), jnp.int32),
            pltpu.VMEM((2 * pre, HD), F32),
            pltpu.VMEM((levels, 2 * pre), BF16),
            pltpu.VMEM((kv, Z, 2 * pre, rows), F32),
            pltpu.VMEM((kv, Z, 2 * pre, rows), F32),
            pltpu.VMEM((kv, Z, 1, rows), F32),
            pltpu.VMEM((kv, Z, 1, rows), F32),
            pltpu.VMEM((kv, Z, 2, rows), F32),
            pltpu.VMEM((kv, Z, levels, rows), F32),
            pltpu.VMEM((kv, Z, levels, rows), F32),
            pltpu.VMEM((kv, Z, 2 * lanes, HD), F32),
            pltpu.VMEM((kv, Z, 2 * lanes, HD), F32),
            pltpu.VMEM((kv, Z, 4, 2 * lanes, HD), F32),
            pltpu.VMEM((kv, Z, rows, HD), F32),
            pltpu.VMEM((kv, 2, 4, rows, HD), BF16),
            pltpu.VMEM((kv, 2, 4, rows, HD), BF16),
            pltpu.VMEM((kv, rows, HD), BF16),
            pltpu.VMEM((kv, 2 * pre, HD), F32),
            pltpu.VMEM((kv, 2 * pre, HD), F32),
            pltpu.VMEM((kv, 2, pre, HD), BF16),
            pltpu.VMEM((kv, 2, pre, HD), BF16),
            pltpu.VMEM((kv, 2, pre, HD), BF16),
            pltpu.VMEM((3, 1, HD), F32),
            pltpu.VMEM((Z, 1, HD), F32),
            pltpu.VMEM((second, 1, HD), F32),
            pltpu.VMEM((third, 1, HD), F32),
            dma((kv * (2 * group + 2),)),
            dma((kv, 2 + group)),
            dma((kv, 2)),
            dma((kv, 2)),
            dma,
            dma,
            dma((kv, 2, 2, 4)),
            dma((kv, 2, 2, 4)),
            dma((kv, Z)),
            dma((kv, Z)),
            dma((kv, Z)),
            dma((kv, Z)),
            dma((kv, 2, 4, 2)),
            dma((kv, 2, 4, 2)),
            dma((kv, 2)),
            dma((kv, 2)),
            dma((Z,)),
            dma((Z,)),
            dma((second,)),
            dma((second,)),
            dma((third,)),
            dma((third,)),
        ],
        compiler_params=pltpu.CompilerParams(
            collective_id=0, has_side_effects=True, vmem_limit_bytes=60 * 1024 * 1024),
    )(counts, rate_table, rate_index, queries, keys, values, grad_out)
    out = pl.pallas_call(
        placed,
        out_shape=tuple(jax.ShapeDtypeStruct(x.shape, x.dtype) for x in out),
        in_specs=[any_] * 4,
        out_specs=(any_,) * 4,
        scratch_shapes=[pltpu.VMEM(x.shape, x.dtype) for x in out] + [dma((2, 4))],
        compiler_params=pltpu.CompilerParams(vmem_limit_bytes=60 * 1024 * 1024),
    )(*out)
    return out[0], out[1], out[2], out[3].reshape(levels)


def solution(mesh):
    split = P("req", "ctx", "head")
    return jax.shard_map(
        shards,
        mesh=mesh,
        in_specs=(split, split, split, split, P("req"), P(), P("req", "ctx")),
        out_specs=(split, split, split, P()),
        check_vma=False,
    )
```

```python
import functools

import jax
import jax.numpy as jnp
from jax import lax
from jax.experimental import pallas as pl
from jax.experimental.pallas import tpu as pltpu
from jax.sharding import PartitionSpec as P

HD = 128
Z = 8
SCALE = 128.0 ** (-0.5)
LOG2E = 1.4426950408889634
MESH = pl.DeviceIdType.MESH
F32 = jnp.float32
BF16 = jnp.bfloat16
NT = (((1,), (1,)), ((), ()))
TN = (((0,), (0,)), ((), ()))
NN = (((1,), (0,)), ((), ()))
NEAR = (6, 2, 7, 1)
FAR = (4, 5, 3)
SHORT = (0, 1)


def kernel(
    n_head, n_req, cand, pre, group, kv, levels,
    counts_ref, table_ref, index_ref, q_hbm, k_hbm, v_hbm, o_hbm,
    dq_hbm, dk_hbm, dv_hbm, dt_ref,
    qo, ks, vs, kt, idx_par, bias, onehot,
    probs, dprobs, peaks, deltas, fin, lev_a, lev_b, st_loc, st_in, st_all,
    dq_all, rs_out, rs_in, dq_done, dk_acc, dv_acc, kv_out, kv_in, kv_done,
    t_mid, t_in1, t_in2, t_in3,
    in_sem, out_sem, kv_send, kv_recv, ix_send, ix_recv,
    ag_send, ag_recv, sa_send, sa_recv, sb_send, sb_recv,
    rs_send, rs_recv, dk_send, dk_recv,
    t1_send, t1_recv, t2_send, t2_recv, t3_send, t3_recv,
):
    rows = group * cand
    half = rows // 2
    lanes = rows // HD
    n_core = min(n_req, 2)
    n_hi = n_req // n_core
    ctx = lax.axis_index("ctx")
    head = lax.axis_index("head")
    req = lax.axis_index("req")
    y = ctx // Z
    z = ctx % Z
    hi = req // n_core
    core = req % n_core

    def along_z(by):
        return {"ctx": y * Z + (z + by) % Z}

    partner = {"ctx": (1 - y) * Z + z}
    right, left = along_z(1), along_z(Z - 1)
    far_right, far_left = along_z(2), along_z(Z - 2)
    t2_codes = [(a, b) for a in range(n_head) for b in range(n_core)][1:]
    t3_codes = [(a, b) for a in range(2) for b in range(n_hi)][1:]

    def t2_peer(a, b):
        return {"head": (head + a) % n_head, "req": hi * n_core + (core + b) % n_core}

    def t3_peer(a, b):
        return {
            "ctx": ((y + a) % 2) * Z + z, "req": ((hi + b) % n_hi) * n_core + core}

    barrier = pltpu.get_barrier_semaphore()
    peers = [left, right]
    peers += [t2_peer(*code) for code in t2_codes] + [t3_peer(*code) for code in t3_codes]
    for peer in peers:
        pl.semaphore_signal(barrier, inc=1, device_id=peer, device_id_type=MESH)

    loads, late_loads = [], []
    for g in range(kv):
        for j in range(group):
            lo = (g * group + j) * HD
            for part, src in ((0, q_hbm), (1, o_hbm)):
                loads.append(pltpu.make_async_copy(
                    src.at[0, :, pl.ds(lo, HD)],
                    qo.at[0, g, part, pl.ds(j * cand, cand), :],
                    in_sem.at[len(loads)]))
    for g in range(kv):
        for src, dst in ((k_hbm, ks), (v_hbm, vs)):
            late_loads.append(pltpu.make_async_copy(
                src.at[0, :, pl.ds(g * HD, HD)],
                dst.at[g, pl.ds(0, pre), :],
                in_sem.at[len(loads) + len(late_loads)]))
    for copy in loads + late_loads:
        copy.start()

    dk_acc[...] = jnp.zeros_like(dk_acc)
    dv_acc[...] = jnp.zeros_like(dv_acc)

    level = lax.broadcasted_iota(jnp.int32, (levels, HD), 0)
    table = jnp.zeros((levels, HD), F32)
    for i in range(levels):
        table = jnp.where(level == i, table_ref[i], table)
    table = table.astype(BF16)

    def offsets(index, place):
        hot = (lax.broadcasted_iota(jnp.int32, (levels, pre), 0) == index)
        hot = hot.astype(F32).astype(BF16)
        onehot[:, pl.ds(place * pre, pre)] = hot
        bias[pl.ds(place * pre, pre), :] = lax.dot_general(
            hot, table, TN, preferred_element_type=F32) * LOG2E

    offsets(index_ref[...], 0)

    for copy in loads + late_loads:
        copy.wait()
    live = counts_ref[0] - ctx * cand
    slot = lax.rem(lax.broadcasted_iota(jnp.int32, (rows, HD), 0), cand)
    for g in range(kv):
        qo[0, g, 1] = jnp.where(slot < live, qo[0, g, 1], jnp.zeros((rows, HD), BF16))

    pl.semaphore_wait(barrier, len(peers))

    def remote(src, dst, send, recv, device):
        return pltpu.make_async_remote_copy(
            src_ref=src, dst_ref=dst, send_sem=send, recv_sem=recv,
            device_id=device, device_id_type=MESH)

    def gather(g, way, step, part):
        if way == 0:
            src, dst, device = lax.rem(9 - step, Z), Z - step, right
        else:
            src, dst, device = step - 1, step, left
        return remote(
            qo.at[src, g, part], qo.at[dst, g, part],
            ag_send.at[g, way, part, step - 1], ag_recv.at[g, way, part, step - 1], device)

    def kv_copy(g, which):
        ref = (ks, vs)[which]
        return remote(
            ref.at[g, pl.ds(0, pre), :], ref.at[g, pl.ds(pre, pre), :],
            kv_send.at[g, which], kv_recv.at[g, which], partner)

    ix_copy = remote(index_ref, idx_par, ix_send, ix_recv, partner)

    def stat_a(g, o):
        return remote(
            st_loc.at[g, o], st_in.at[g, o],
            sa_send.at[g, o], sa_recv.at[g, o], along_z(o))

    def stat_b(g, o):
        return remote(
            st_all.at[g, 0], st_all.at[g, o],
            sb_send.at[g, o], sb_recv.at[g, o], along_z(o))

    def scatter(g, way, step, part):
        at = pl.ds(part * half, half)
        return remote(
            rs_out.at[g, way, step, at, :], rs_in.at[g, way, step, at, :],
            rs_send.at[g, way, step, part], rs_recv.at[g, way, step, part],
            (far_left, far_right)[way] if step == 0 and g in SHORT else (left, right)[way])

    def kv_grad(g, which):
        return remote(
            kv_out.at[g, which], kv_in.at[g, which],
            dk_send.at[g, which], dk_recv.at[g, which], partner)

    def t1_copy(o):
        return remote(
            t_mid.at[0], t_in1.at[o], t1_send.at[o], t1_recv.at[o], along_z(o))

    def t2_copy(i):
        return remote(
            t_mid.at[1], t_in2.at[i], t2_send.at[i], t2_recv.at[i], t2_peer(*t2_codes[i]))

    def t3_copy(i):
        return remote(
            t_mid.at[2], t_in3.at[i], t3_send.at[i], t3_recv.at[i], t3_peer(*t3_codes[i]))

    for g in range(kv):
        for part in range(2):
            for way in range(2):
                gather(g, way, 1, part).start()
        if g == 0:
            ix_copy.start()
        for which in range(2):
            kv_copy(g, which).start()

    def split(row):
        return [row[:, i * HD:(i + 1) * HD] for i in range(lanes)]

    def joined(block):
        return jnp.concatenate([block[i:i + 1] for i in range(lanes)], axis=1)

    def first_pass(g, s):
        q_blk = qo[s, g, 0]
        o_blk = qo[s, g, 1]
        off = jnp.concatenate([bias[...]] * lanes, axis=1)
        scores = lax.dot_general(ks[g], q_blk, NT, preferred_element_type=F32)
        scores = scores * (SCALE * LOG2E) + off
        peak = jnp.max(scores, axis=0, keepdims=True)
        prob = jnp.exp2(scores - peak)
        total = jnp.sum(prob, axis=0, keepdims=True)
        dprob = lax.dot_general(vs[g], o_blk, NT, preferred_element_type=F32)
        delta = jnp.sum(prob * dprob, axis=0, keepdims=True) / total
        probs[g, s] = prob
        dprobs[g, s] = dprob
        peaks[g, s] = peak
        deltas[g, s] = delta
        lev_a[g, s] = lax.dot_general(
            onehot[...], (prob * (dprob - delta)).astype(BF16), NN,
            preferred_element_type=F32)
        lev_b[g, s] = lax.dot_general(
            onehot[...], prob.astype(BF16), NN, preferred_element_type=F32)
        lse = peak + jnp.log2(total)
        st_loc[g, s] = jnp.concatenate(split(lse) + split(delta), axis=0)

    def merged(parts):
        lse = [p[0:lanes] for p in parts]
        top = functools.reduce(jnp.maximum, lse)
        total = top + jnp.log2(sum(jnp.exp2(v - top) for v in lse))
        delta = sum(jnp.exp2(v - total) * p[lanes:] for v, p in zip(lse, parts))
        return total, delta

    def combine(g):
        total, delta = merged([st_loc[g, 0]] + [st_in[g, o] for o in NEAR])
        st_all[g, 0, 0] = jnp.concatenate([total, delta], axis=0)

    def finish(g):
        acc = []
        for s in range(Z):
            total, delta = merged([st_all[g, (Z - s) % Z, 0]] + [
                st_all[g, (Z + o - s) % Z, 1 + i] for i, o in enumerate(FAR)])
            delta = joined(delta)
            factor = jnp.exp2(peaks[g, s] - joined(total))
            fin[g, s] = jnp.concatenate([factor, delta], axis=0)
            term = factor * (lev_a[g, s] - (delta - deltas[g, s]) * lev_b[g, s])
            acc += split(term)
        return sum(acc)

    def second_pass(g, s):
        both = fin[g, s]
        prob = probs[g, s] * both[0:1]
        dscore = prob * (dprobs[g, s] - both[1:2])
        prob_b = prob.astype(BF16)
        dscore_b = dscore.astype(BF16)
        dq = lax.dot_general(kt[g], dscore_b, NN, preferred_element_type=F32)
        dq_all[g, s] = dq.T
        dv_acc[g] += lax.dot_general(prob_b, qo[s, g, 1], NN, preferred_element_type=F32)
        dk_acc[g] += lax.dot_general(dscore_b, qo[s, g, 0], NN, preferred_element_type=F32)

    def kv_finish(g):
        for which, acc in ((0, dk_acc), (1, dv_acc)):
            kv_grad(g, which).wait_recv()
            total = acc[g, 0:pre] + kv_in[g, which].astype(F32)
            if which == 0:
                total = total * SCALE
            kv_done[g, which] = total.astype(BF16)
            kv_store(g, which).start()

    def kv_store(g, which):
        hbm = (dk_hbm, dv_hbm)[which]
        return pltpu.make_async_copy(
            kv_done.at[g, which], hbm.at[0, :, pl.ds(g * HD, HD)], out_sem.at[g, which])

    def dq_store(g, j):
        return pltpu.make_async_copy(
            dq_done.at[g, pl.ds(j * cand, cand), :],
            dq_hbm.at[0, :, pl.ds((g * group + j) * HD, HD)],
            out_sem.at[g, 2 + j])

    def gather_tick(t, _):
        k, g = 1 + t // kv, t % kv

        @pl.when(k < 4)
        def _():
            for part in range(2):
                for way in range(2):
                    gather(g, way, k, part).wait_recv()

                    @pl.when((k < 3) | (part == way))
                    def _():
                        gather(g, way, k + 1, part).start()

        @pl.when(k == 4)
        def _():
            for o in NEAR:
                stat_a(g, o).wait()
            combine(g)
            gather(g, 0, 4, 0).wait_recv()
            gather(g, 1, 4, 1).wait_recv()

        for i in range(kv):
            @pl.when((k == 1) & (g == i))
            def _():
                if i == 0:
                    ix_copy.wait()
                    offsets(idx_par[...], 1)
                for which in range(2):
                    kv_copy(i, which).wait()
                kt[i] = ks[i].astype(F32).T.astype(BF16)

        def chunk(c, _):
            first_pass(g, jnp.where(c == 0, Z - k, jnp.where(c == 1, k, 0)))
            return 0

        lax.fori_loop(0, jnp.where(k == 4, 1, jnp.where(k == 1, 3, 2)), chunk, 0)

        @pl.when(k == 2)
        def _():
            for o in NEAR:
                stat_a(g, o).start()

        @pl.when(k == 4)
        def _():
            for i, o in enumerate(FAR):
                st_all[g, 0, 1 + i] = st_loc[g, o]
            for o in (4, 5, 3, 6, 2, 7, 1):
                stat_b(g, o).start()

        return 0

    lax.fori_loop(0, 4 * kv, gather_tick, 0)

    def stats(g):
        for o in (1, 7, 2, 6, 3, 5, 4):
            stat_b(g, o).wait()
        term = finish(g)
        place = lax.broadcasted_iota(jnp.int32, (levels, HD), 0)
        across = lax.broadcasted_iota(jnp.int32, (levels, HD), 1)
        term = jnp.sum(term, axis=1, keepdims=True)
        term = jnp.sum(jnp.where(place == across, term, 0.0), axis=0, keepdims=True)
        t_mid[0] = term if g == 0 else t_mid[0] + term

    def table_first():
        for o in range(1, Z):
            t1_copy(o).start()

    def table_second():
        for o in range(1, Z):
            t1_copy(o).wait()
        t_mid[1] = t_mid[0] + sum(t_in1[o] for o in range(1, Z))
        for i in range(len(t2_codes)):
            t2_copy(i).start()

    def table_third():
        for i in range(len(t2_codes)):
            t2_copy(i).wait()
        t_mid[2] = t_mid[1] + sum(t_in2[i] for i in range(len(t2_codes)))
        for i in range(len(t3_codes)):
            t3_copy(i).start()

    def scatter_first(g):
        for way in range(2):
            at = pl.ds(way * half, half)
            rs_out[g, way, 0, at, :] = dq_all[g, 4, at, :].astype(BF16)
            scatter(g, way, 0, way).start()

    def scatter_next(g, step):
        for part in range(2):
            for way in range(2):
                at = pl.ds(part * half, half)
                dq = dq_all[g, 4 + step if way == 0 else 4 - step, at, :]
                if step == (2 if g in SHORT else 1) and part == way:
                    scatter(g, way, 0, part).wait_recv()
                    dq = dq + rs_in[g, way, 0, at, :].astype(F32)
                if step > 1:
                    scatter(g, way, step - 1, part).wait_recv()
                    dq = dq + rs_in[g, way, step - 1, at, :].astype(F32)
                rs_out[g, way, step, at, :] = dq.astype(BF16)
                scatter(g, way, step, part).start()

    def scatter_last(g):
        for part in range(2):
            at = pl.ds(part * half, half)
            for way in range(2):
                scatter(g, way, 3, part).wait_recv()
            dq = (dq_all[g, 0, at, :] + rs_in[g, 0, 3, at, :].astype(F32)
                  + rs_in[g, 1, 3, at, :].astype(F32))
            dq_done[g, at, :] = (dq * SCALE).astype(BF16)
        for j in range(group):
            dq_store(g, j).start()

    def kv_send_off(g):
        for which, acc in ((0, dk_acc), (1, dv_acc)):
            kv_out[g, which] = acc[g, pre:2 * pre].astype(BF16)
            kv_grad(g, which).start()

    order = [(0, 4), (0, 5), (0, 3), (1, 4), (1, 5), (1, 3), (0, 6), (0, 2), (1, 6), (1, 2),
             (0, 7), (0, 1), (0, 0), (1, 7), (1, 1), (1, 0)]
    before = {0: [lambda: stats(0)], 3: [lambda: stats(1), table_first]}
    after = {
        0: [lambda: scatter_first(0)],
        2: [lambda: scatter_next(0, 1)],
        3: [lambda: scatter_first(1)],
        5: [lambda: scatter_next(1, 1)],
        11: [lambda: scatter_next(0, 2)],
        12: [lambda: kv_send_off(0)],
        14: [lambda: scatter_next(1, 2), table_second],
        15: [lambda: kv_send_off(1)],
    }

    def grad_tick(e, _):
        for at, calls in before.items():
            @pl.when(e == at)
            def _():
                for call in calls:
                    call()

        g = jnp.int32(0)
        s = jnp.int32(0)
        for i, (a, b) in enumerate(order):
            g = jnp.where(e == i, a, g)
            s = jnp.where(e == i, b, s)
        second_pass(g, s)

        for at, calls in after.items():
            @pl.when(e == at)
            def _():
                for call in calls:
                    call()
        return 0

    lax.fori_loop(0, len(order), grad_tick, 0)

    scatter_next(0, 3)
    scatter_next(1, 3)
    table_third()
    kv_finish(0)
    scatter_last(0)

    for g in range(kv):
        for way in range(2):
            for part in range(2):
                for step in range(1, 5):
                    if step < 4 or part == way:
                        gather(g, way, step, part).wait_send()
                for step in range(4):
                    if step > 0 or part == way:
                        scatter(g, way, step, part).wait_send()
        for which in range(2):
            kv_grad(g, which).wait_send()

    kv_finish(1)
    scatter_last(1)
    for i in range(len(t3_codes)):
        t3_copy(i).wait()
    total = t_mid[2] + sum(t_in3[i] for i in range(len(t3_codes)))
    dt_ref[...] = total[:, 0:levels]

    for g in range(kv):
        for which in range(2):
            kv_store(g, which).wait()
        for j in range(group):
            dq_store(g, j).wait()


def placed(*refs):
    copies = [
        pltpu.make_async_copy(refs[i], refs[4 + i], refs[8].at[i]) for i in range(4)]
    for copy in copies:
        copy.start()
    for copy in copies:
        copy.wait()


def shards(queries, keys, values, grad_out, counts, rate_table, rate_index):
    n_head, n_req = lax.axis_size("head"), lax.axis_size("req")
    cand, pre = queries.shape[1], keys.shape[1]
    kv = keys.shape[2] // HD
    group = queries.shape[2] // keys.shape[2]
    levels = rate_table.shape[0]
    rows = group * cand
    lanes = rows // HD
    second = max(n_head * min(n_req, 2) - 1, 1)
    third = 2 * (n_req // min(n_req, 2)) - 1
    any_ = pl.BlockSpec(memory_space=pl.ANY)
    smem = pl.BlockSpec(memory_space=pltpu.SMEM)
    vmem = pl.BlockSpec(memory_space=pltpu.VMEM)
    dma = pltpu.SemaphoreType.DMA
    out = pl.pallas_call(
        functools.partial(kernel, n_head, n_req, cand, pre, group, kv, levels),
        out_shape=(
            jax.ShapeDtypeStruct(queries.shape, BF16),
            jax.ShapeDtypeStruct(keys.shape, BF16),
            jax.ShapeDtypeStruct(values.shape, BF16),
            jax.ShapeDtypeStruct((1, levels), F32),
        ),
        in_specs=[smem, smem, vmem, any_, any_, any_, any_],
        out_specs=(any_, any_, any_, vmem),
        scratch_shapes=[
            pltpu.VMEM((Z, kv, 2, rows, HD), BF16),
            pltpu.VMEM((kv, 2 * pre, HD), BF16),
            pltpu.VMEM((kv, 2 * pre, HD), BF16),
            pltpu.VMEM((kv, HD, 2 * pre), BF16),
            pltpu.VMEM((1, pre), jnp.int32),
            pltpu.VMEM((2 * pre, HD), F32),
            pltpu.VMEM((levels, 2 * pre), BF16),
            pltpu.VMEM((kv, Z, 2 * pre, rows), F32),
            pltpu.VMEM((kv, Z, 2 * pre, rows), F32),
            pltpu.VMEM((kv, Z, 1, rows), F32),
            pltpu.VMEM((kv, Z, 1, rows), F32),
            pltpu.VMEM((kv, Z, 2, rows), F32),
            pltpu.VMEM((kv, Z, levels, rows), F32),
            pltpu.VMEM((kv, Z, levels, rows), F32),
            pltpu.VMEM((kv, Z, 2 * lanes, HD), F32),
            pltpu.VMEM((kv, Z, 2 * lanes, HD), F32),
            pltpu.VMEM((kv, Z, 4, 2 * lanes, HD), F32),
            pltpu.VMEM((kv, Z, rows, HD), F32),
            pltpu.VMEM((kv, 2, 4, rows, HD), BF16),
            pltpu.VMEM((kv, 2, 4, rows, HD), BF16),
            pltpu.VMEM((kv, rows, HD), BF16),
            pltpu.VMEM((kv, 2 * pre, HD), F32),
            pltpu.VMEM((kv, 2 * pre, HD), F32),
            pltpu.VMEM((kv, 2, pre, HD), BF16),
            pltpu.VMEM((kv, 2, pre, HD), BF16),
            pltpu.VMEM((kv, 2, pre, HD), BF16),
            pltpu.VMEM((3, 1, HD), F32),
            pltpu.VMEM((Z, 1, HD), F32),
            pltpu.VMEM((second, 1, HD), F32),
            pltpu.VMEM((third, 1, HD), F32),
            dma((kv * (2 * group + 2),)),
            dma((kv, 2 + group)),
            dma((kv, 2)),
            dma((kv, 2)),
            dma,
            dma,
            dma((kv, 2, 2, 4)),
            dma((kv, 2, 2, 4)),
            dma((kv, Z)),
            dma((kv, Z)),
            dma((kv, Z)),
            dma((kv, Z)),
            dma((kv, 2, 4, 2)),
            dma((kv, 2, 4, 2)),
            dma((kv, 2)),
            dma((kv, 2)),
            dma((Z,)),
            dma((Z,)),
            dma((second,)),
            dma((second,)),
            dma((third,)),
            dma((third,)),
        ],
        compiler_params=pltpu.CompilerParams(
            collective_id=0, has_side_effects=True, vmem_limit_bytes=54784 * 1024),
    )(counts, rate_table, rate_index, queries, keys, values, grad_out)
    out = pl.pallas_call(
        placed,
        out_shape=tuple(jax.ShapeDtypeStruct(x.shape, x.dtype) for x in out),
        in_specs=[any_] * 4,
        out_specs=(any_,) * 4,
        scratch_shapes=[dma((4,))],
        compiler_params=pltpu.CompilerParams(vmem_limit_bytes=16 * 1024 * 1024),
    )(*out)
    return out[0], out[1], out[2], out[3].reshape(levels)


def solution(mesh):
    split = P("req", "ctx", "head")
    return jax.shard_map(
        shards,
        mesh=mesh,
        in_specs=(split, split, split, split, P("req"), P(), P("req", "ctx")),
        out_specs=(split, split, split, P()),
        check_vma=False,
    )
```

```python
import functools

import jax
import jax.numpy as jnp
from jax import lax
from jax.experimental import pallas as pl
from jax.experimental.pallas import tpu as pltpu
from jax.sharding import PartitionSpec as P

HD = 128
Z = 8
SCALE = 128.0 ** (-0.5)
LOG2E = 1.4426950408889634
MESH = pl.DeviceIdType.MESH
F32 = jnp.float32
BF16 = jnp.bfloat16
NT = (((1,), (1,)), ((), ()))
TN = (((0,), (0,)), ((), ()))
NN = (((1,), (0,)), ((), ()))
NEAR = (6, 2, 7, 1)
FAR = (4, 5, 3)
SHORT = (0, 1)


def kernel(
    n_head, n_req, cand, pre, group, kv, levels,
    counts_ref, table_ref, index_ref, q_hbm, k_hbm, v_hbm, o_hbm,
    dq_hbm, dk_hbm, dv_hbm, dt_ref,
    qo, ks, vs, kt, idx_par, bias, onehot,
    probs, dprobs, peaks, deltas, fin, lev_a, lev_b, st_loc, st_in, st_all,
    dq_all, rs_out, rs_in, dq_done, dk_acc, dv_acc, kv_out, kv_in, kv_done,
    t_mid, t_in1, t_in2, t_in3,
    in_sem, out_sem, kv_send, kv_recv, ix_send, ix_recv,
    ag_send, ag_recv, sa_send, sa_recv, sb_send, sb_recv,
    rs_send, rs_recv, dk_send, dk_recv,
    t1_send, t1_recv, t2_send, t2_recv, t3_send, t3_recv,
):
    rows = group * cand
    half = rows // 2
    lanes = rows // HD
    n_core = min(n_req, 2)
    n_hi = n_req // n_core
    ctx = lax.axis_index("ctx")
    head = lax.axis_index("head")
    req = lax.axis_index("req")
    y = ctx // Z
    z = ctx % Z
    hi = req // n_core
    core = req % n_core

    def along_z(by):
        return {"ctx": y * Z + (z + by) % Z}

    partner = {"ctx": (1 - y) * Z + z}
    right, left = along_z(1), along_z(Z - 1)
    far_right, far_left = along_z(2), along_z(Z - 2)
    t2_codes = [(a, b) for a in range(n_head) for b in range(n_core)][1:]
    t3_codes = [(a, b) for a in range(2) for b in range(n_hi)][1:]

    def t2_peer(a, b):
        return {"head": (head + a) % n_head, "req": hi * n_core + (core + b) % n_core}

    def t3_peer(a, b):
        return {
            "ctx": ((y + a) % 2) * Z + z, "req": ((hi + b) % n_hi) * n_core + core}

    barrier = pltpu.get_barrier_semaphore()
    peers = [left, right]
    peers += [t2_peer(*code) for code in t2_codes] + [t3_peer(*code) for code in t3_codes]
    for peer in peers:
        pl.semaphore_signal(barrier, inc=1, device_id=peer, device_id_type=MESH)

    loads, late_loads = [], []
    for g in range(kv):
        for j in range(group):
            lo = (g * group + j) * HD
            for part, src in ((0, q_hbm), (1, o_hbm)):
                loads.append(pltpu.make_async_copy(
                    src.at[0, :, pl.ds(lo, HD)],
                    qo.at[0, g, part, pl.ds(j * cand, cand), :],
                    in_sem.at[len(loads)]))
    for g in range(kv):
        for src, dst in ((k_hbm, ks), (v_hbm, vs)):
            late_loads.append(pltpu.make_async_copy(
                src.at[0, :, pl.ds(g * HD, HD)],
                dst.at[g, pl.ds(0, pre), :],
                in_sem.at[len(loads) + len(late_loads)]))
    for copy in loads + late_loads:
        copy.start()

    pl.semaphore_wait(barrier, len(peers))

    def remote(src, dst, send, recv, device):
        return pltpu.make_async_remote_copy(
            src_ref=src, dst_ref=dst, send_sem=send, recv_sem=recv,
            device_id=device, device_id_type=MESH)

    def gather(g, way, step, part):
        if way == 0:
            src, dst, device = lax.rem(9 - step, Z), Z - step, right
        else:
            src, dst, device = step - 1, step, left
        return remote(
            qo.at[src, g, part], qo.at[dst, g, part],
            ag_send.at[g, way, part, step - 1], ag_recv.at[g, way, part, step - 1], device)

    def kv_copy(g, which):
        ref = (ks, vs)[which]
        return remote(
            ref.at[g, pl.ds(0, pre), :], ref.at[g, pl.ds(pre, pre), :],
            kv_send.at[g, which], kv_recv.at[g, which], partner)

    ix_copy = remote(index_ref, idx_par, ix_send, ix_recv, partner)

    def stat_a(g, o):
        return remote(
            st_loc.at[g, o], st_in.at[g, o],
            sa_send.at[g, o], sa_recv.at[g, o], along_z(o))

    def stat_b(g, o):
        return remote(
            st_all.at[g, 0], st_all.at[g, o],
            sb_send.at[g, o], sb_recv.at[g, o], along_z(o))

    def scatter(g, way, step, part):
        at = pl.ds(part * half, half)
        return remote(
            rs_out.at[g, way, step, at, :], rs_in.at[g, way, step, at, :],
            rs_send.at[g, way, step, part], rs_recv.at[g, way, step, part],
            (far_left, far_right)[way] if step == 0 and g in SHORT else (left, right)[way])

    def kv_grad(g, which):
        return remote(
            kv_out.at[g, which], kv_in.at[g, which],
            dk_send.at[g, which], dk_recv.at[g, which], partner)

    def t1_copy(o):
        return remote(
            t_mid.at[0], t_in1.at[o], t1_send.at[o], t1_recv.at[o], along_z(o))

    def t2_copy(i):
        return remote(
            t_mid.at[1], t_in2.at[i], t2_send.at[i], t2_recv.at[i], t2_peer(*t2_codes[i]))

    def t3_copy(i):
        return remote(
            t_mid.at[2], t_in3.at[i], t3_send.at[i], t3_recv.at[i], t3_peer(*t3_codes[i]))

    live = counts_ref[0] - ctx * cand
    slot = lax.rem(lax.broadcasted_iota(jnp.int32, (rows, HD), 0), cand)
    for g in range(kv):
        for part in range(2):
            for j in range(group):
                loads[2 * (g * group + j) + part].wait()
            if part == 1:
                qo[0, g, 1] = jnp.where(
                    slot < live, qo[0, g, 1], jnp.zeros((rows, HD), BF16))
            for way in range(2):
                gather(g, way, 1, part).start()
    ix_copy.start()
    for g in range(kv):
        for which in range(2):
            late_loads[2 * g + which].wait()
            kv_copy(g, which).start()

    dk_acc[...] = jnp.zeros_like(dk_acc)
    dv_acc[...] = jnp.zeros_like(dv_acc)

    level = lax.broadcasted_iota(jnp.int32, (levels, HD), 0)
    table = jnp.zeros((levels, HD), F32)
    for i in range(levels):
        table = jnp.where(level == i, table_ref[i], table)
    table = table.astype(BF16)

    def offsets(index, place):
        hot = (lax.broadcasted_iota(jnp.int32, (levels, pre), 0) == index)
        hot = hot.astype(F32).astype(BF16)
        onehot[:, pl.ds(place * pre, pre)] = hot
        bias[pl.ds(place * pre, pre), :] = lax.dot_general(
            hot, table, TN, preferred_element_type=F32) * LOG2E

    offsets(index_ref[...], 0)

    def split(row):
        return [row[:, i * HD:(i + 1) * HD] for i in range(lanes)]

    def joined(block):
        return jnp.concatenate([block[i:i + 1] for i in range(lanes)], axis=1)

    def first_pass(g, s):
        q_blk = qo[s, g, 0]
        o_blk = qo[s, g, 1]
        off = jnp.concatenate([bias[...]] * lanes, axis=1)
        scores = lax.dot_general(ks[g], q_blk, NT, preferred_element_type=F32)
        scores = scores * (SCALE * LOG2E) + off
        peak = jnp.max(scores, axis=0, keepdims=True)
        prob = jnp.exp2(scores - peak)
        total = jnp.sum(prob, axis=0, keepdims=True)
        dprob = lax.dot_general(vs[g], o_blk, NT, preferred_element_type=F32)
        delta = jnp.sum(prob * dprob, axis=0, keepdims=True) / total
        probs[g, s] = prob
        dprobs[g, s] = dprob
        peaks[g, s] = peak
        deltas[g, s] = delta
        lev_a[g, s] = lax.dot_general(
            onehot[...], (prob * (dprob - delta)).astype(BF16), NN,
            preferred_element_type=F32)
        lev_b[g, s] = lax.dot_general(
            onehot[...], prob.astype(BF16), NN, preferred_element_type=F32)
        lse = peak + jnp.log2(total)
        st_loc[g, s] = jnp.concatenate(split(lse) + split(delta), axis=0)

    def merged(parts):
        lse = [p[0:lanes] for p in parts]
        top = functools.reduce(jnp.maximum, lse)
        total = top + jnp.log2(sum(jnp.exp2(v - top) for v in lse))
        delta = sum(jnp.exp2(v - total) * p[lanes:] for v, p in zip(lse, parts))
        return total, delta

    def combine(g):
        total, delta = merged([st_loc[g, 0]] + [st_in[g, o] for o in NEAR])
        st_all[g, 0, 0] = jnp.concatenate([total, delta], axis=0)

    def finish(g):
        acc = []
        for s in range(Z):
            total, delta = merged([st_all[g, (Z - s) % Z, 0]] + [
                st_all[g, (Z + o - s) % Z, 1 + i] for i, o in enumerate(FAR)])
            delta = joined(delta)
            factor = jnp.exp2(peaks[g, s] - joined(total))
            fin[g, s] = jnp.concatenate([factor, delta], axis=0)
            term = factor * (lev_a[g, s] - (delta - deltas[g, s]) * lev_b[g, s])
            acc += split(term)
        return sum(acc)

    def second_pass(g, s):
        both = fin[g, s]
        prob = probs[g, s] * both[0:1]
        dscore = prob * (dprobs[g, s] - both[1:2])
        prob_b = prob.astype(BF16)
        dscore_b = dscore.astype(BF16)
        dq = lax.dot_general(kt[g], dscore_b, NN, preferred_element_type=F32)
        dq_all[g, s] = dq.T
        dv_acc[g] += lax.dot_general(prob_b, qo[s, g, 1], NN, preferred_element_type=F32)
        dk_acc[g] += lax.dot_general(dscore_b, qo[s, g, 0], NN, preferred_element_type=F32)

    def kv_finish(g):
        for which, acc in ((0, dk_acc), (1, dv_acc)):
            kv_grad(g, which).wait_recv()
            total = acc[g, 0:pre] + kv_in[g, which].astype(F32)
            if which == 0:
                total = total * SCALE
            kv_done[g, which] = total.astype(BF16)
            kv_store(g, which).start()

    def kv_store(g, which):
        hbm = (dk_hbm, dv_hbm)[which]
        return pltpu.make_async_copy(
            kv_done.at[g, which], hbm.at[0, :, pl.ds(g * HD, HD)], out_sem.at[g, which])

    def dq_store(g, j):
        return pltpu.make_async_copy(
            dq_done.at[g, pl.ds(j * cand, cand), :],
            dq_hbm.at[0, :, pl.ds((g * group + j) * HD, HD)],
            out_sem.at[g, 2 + j])

    def gather_tick(t, _):
        k, g = 1 + t // kv, t % kv

        @pl.when(k < 4)
        def _():
            for part in range(2):
                for way in range(2):
                    gather(g, way, k, part).wait_recv()

                    @pl.when((k < 3) | (part == way))
                    def _():
                        gather(g, way, k + 1, part).start()

        @pl.when(k == 4)
        def _():
            for o in NEAR:
                stat_a(g, o).wait()
            combine(g)
            gather(g, 0, 4, 0).wait_recv()
            gather(g, 1, 4, 1).wait_recv()

        for i in range(kv):
            @pl.when((k == 1) & (g == i))
            def _():
                if i == 0:
                    ix_copy.wait()
                    offsets(idx_par[...], 1)
                for which in range(2):
                    kv_copy(i, which).wait()
                kt[i] = ks[i].astype(F32).T.astype(BF16)

        def chunk(c, _):
            first_pass(g, jnp.where(c == 0, Z - k, jnp.where(c == 1, k, 0)))
            return 0

        lax.fori_loop(0, jnp.where(k == 4, 1, jnp.where(k == 1, 3, 2)), chunk, 0)

        @pl.when(k == 2)
        def _():
            for o in NEAR:
                stat_a(g, o).start()

        @pl.when(k == 4)
        def _():
            for i, o in enumerate(FAR):
                st_all[g, 0, 1 + i] = st_loc[g, o]
            for o in (4, 5, 3, 6, 2, 7, 1):
                stat_b(g, o).start()

        return 0

    lax.fori_loop(0, 4 * kv, gather_tick, 0)

    def stats(g):
        for o in (1, 7, 2, 6, 3, 5, 4):
            stat_b(g, o).wait()
        term = finish(g)
        place = lax.broadcasted_iota(jnp.int32, (levels, HD), 0)
        across = lax.broadcasted_iota(jnp.int32, (levels, HD), 1)
        term = jnp.sum(term, axis=1, keepdims=True)
        term = jnp.sum(jnp.where(place == across, term, 0.0), axis=0, keepdims=True)
        t_mid[0] = term if g == 0 else t_mid[0] + term

    def table_first():
        for o in range(1, Z):
            t1_copy(o).start()

    def table_second():
        for o in range(1, Z):
            t1_copy(o).wait()
        t_mid[1] = t_mid[0] + sum(t_in1[o] for o in range(1, Z))
        for i in range(len(t2_codes)):
            t2_copy(i).start()

    def table_third():
        for i in range(len(t2_codes)):
            t2_copy(i).wait()
        t_mid[2] = t_mid[1] + sum(t_in2[i] for i in range(len(t2_codes)))
        for i in range(len(t3_codes)):
            t3_copy(i).start()

    def scatter_first(g):
        for way in range(2):
            at = pl.ds(way * half, half)
            rs_out[g, way, 0, at, :] = dq_all[g, 4, at, :].astype(BF16)
            scatter(g, way, 0, way).start()

    def scatter_next(g, step):
        for part in range(2):
            for way in range(2):
                at = pl.ds(part * half, half)
                dq = dq_all[g, 4 + step if way == 0 else 4 - step, at, :]
                if step == (2 if g in SHORT else 1) and part == way:
                    scatter(g, way, 0, part).wait_recv()
                    dq = dq + rs_in[g, way, 0, at, :].astype(F32)
                if step > 1:
                    scatter(g, way, step - 1, part).wait_recv()
                    dq = dq + rs_in[g, way, step - 1, at, :].astype(F32)
                rs_out[g, way, step, at, :] = dq.astype(BF16)
                scatter(g, way, step, part).start()

    def scatter_last(g):
        for part in range(2):
            at = pl.ds(part * half, half)
            for way in range(2):
                scatter(g, way, 3, part).wait_recv()
            dq = (dq_all[g, 0, at, :] + rs_in[g, 0, 3, at, :].astype(F32)
                  + rs_in[g, 1, 3, at, :].astype(F32))
            dq_done[g, at, :] = (dq * SCALE).astype(BF16)
        for j in range(group):
            dq_store(g, j).start()

    def kv_send_off(g):
        for which, acc in ((0, dk_acc), (1, dv_acc)):
            kv_out[g, which] = acc[g, pre:2 * pre].astype(BF16)
            kv_grad(g, which).start()

    order = [(0, 4), (0, 5), (0, 3), (1, 4), (1, 5), (1, 3), (0, 6), (0, 2), (1, 6), (1, 2),
             (0, 7), (0, 1), (0, 0), (1, 7), (1, 1), (1, 0)]
    before = {0: [lambda: stats(0)], 3: [lambda: stats(1), table_first]}
    after = {
        0: [lambda: scatter_first(0)],
        2: [lambda: scatter_next(0, 1)],
        3: [lambda: scatter_first(1)],
        5: [lambda: scatter_next(1, 1)],
        11: [lambda: scatter_next(0, 2)],
        12: [lambda: kv_send_off(0)],
        14: [lambda: scatter_next(1, 2), table_second],
        15: [lambda: kv_send_off(1)],
    }

    def grad_tick(e, _):
        for at, calls in before.items():
            @pl.when(e == at)
            def _():
                for call in calls:
                    call()

        g = jnp.int32(0)
        s = jnp.int32(0)
        for i, (a, b) in enumerate(order):
            g = jnp.where(e == i, a, g)
            s = jnp.where(e == i, b, s)
        second_pass(g, s)

        for at, calls in after.items():
            @pl.when(e == at)
            def _():
                for call in calls:
                    call()
        return 0

    lax.fori_loop(0, len(order), grad_tick, 0)

    scatter_next(0, 3)
    scatter_next(1, 3)
    table_third()
    kv_finish(0)
    scatter_last(0)

    for g in range(kv):
        for way in range(2):
            for part in range(2):
                for step in range(1, 5):
                    if step < 4 or part == way:
                        gather(g, way, step, part).wait_send()
                for step in range(4):
                    if step > 0 or part == way:
                        scatter(g, way, step, part).wait_send()
        for which in range(2):
            kv_grad(g, which).wait_send()

    kv_finish(1)
    scatter_last(1)
    for i in range(len(t3_codes)):
        t3_copy(i).wait()
    total = t_mid[2] + sum(t_in3[i] for i in range(len(t3_codes)))
    dt_ref[...] = total[:, 0:levels]

    for g in range(kv):
        for which in range(2):
            kv_store(g, which).wait()
        for j in range(group):
            dq_store(g, j).wait()


def placed(*refs):
    copies = [
        pltpu.make_async_copy(refs[i], refs[4 + i], refs[8].at[i]) for i in range(4)]
    for copy in copies:
        copy.start()
    for copy in copies:
        copy.wait()


def shards(queries, keys, values, grad_out, counts, rate_table, rate_index):
    n_head, n_req = lax.axis_size("head"), lax.axis_size("req")
    cand, pre = queries.shape[1], keys.shape[1]
    kv = keys.shape[2] // HD
    group = queries.shape[2] // keys.shape[2]
    levels = rate_table.shape[0]
    rows = group * cand
    lanes = rows // HD
    second = max(n_head * min(n_req, 2) - 1, 1)
    third = 2 * (n_req // min(n_req, 2)) - 1
    any_ = pl.BlockSpec(memory_space=pl.ANY)
    smem = pl.BlockSpec(memory_space=pltpu.SMEM)
    vmem = pl.BlockSpec(memory_space=pltpu.VMEM)
    dma = pltpu.SemaphoreType.DMA
    out = pl.pallas_call(
        functools.partial(kernel, n_head, n_req, cand, pre, group, kv, levels),
        out_shape=(
            jax.ShapeDtypeStruct(queries.shape, BF16),
            jax.ShapeDtypeStruct(keys.shape, BF16),
            jax.ShapeDtypeStruct(values.shape, BF16),
            jax.ShapeDtypeStruct((1, levels), F32),
        ),
        in_specs=[smem, smem, vmem, any_, any_, any_, any_],
        out_specs=(any_, any_, any_, vmem),
        scratch_shapes=[
            pltpu.VMEM((Z, kv, 2, rows, HD), BF16),
            pltpu.VMEM((kv, 2 * pre, HD), BF16),
            pltpu.VMEM((kv, 2 * pre, HD), BF16),
            pltpu.VMEM((kv, HD, 2 * pre), BF16),
            pltpu.VMEM((1, pre), jnp.int32),
            pltpu.VMEM((2 * pre, HD), F32),
            pltpu.VMEM((levels, 2 * pre), BF16),
            pltpu.VMEM((kv, Z, 2 * pre, rows), F32),
            pltpu.VMEM((kv, Z, 2 * pre, rows), F32),
            pltpu.VMEM((kv, Z, 1, rows), F32),
            pltpu.VMEM((kv, Z, 1, rows), F32),
            pltpu.VMEM((kv, Z, 2, rows), F32),
            pltpu.VMEM((kv, Z, levels, rows), F32),
            pltpu.VMEM((kv, Z, levels, rows), F32),
            pltpu.VMEM((kv, Z, 2 * lanes, HD), F32),
            pltpu.VMEM((kv, Z, 2 * lanes, HD), F32),
            pltpu.VMEM((kv, Z, 4, 2 * lanes, HD), F32),
            pltpu.VMEM((kv, Z, rows, HD), F32),
            pltpu.VMEM((kv, 2, 4, rows, HD), BF16),
            pltpu.VMEM((kv, 2, 4, rows, HD), BF16),
            pltpu.VMEM((kv, rows, HD), BF16),
            pltpu.VMEM((kv, 2 * pre, HD), F32),
            pltpu.VMEM((kv, 2 * pre, HD), F32),
            pltpu.VMEM((kv, 2, pre, HD), BF16),
            pltpu.VMEM((kv, 2, pre, HD), BF16),
            pltpu.VMEM((kv, 2, pre, HD), BF16),
            pltpu.VMEM((3, 1, HD), F32),
            pltpu.VMEM((Z, 1, HD), F32),
            pltpu.VMEM((second, 1, HD), F32),
            pltpu.VMEM((third, 1, HD), F32),
            dma((kv * (2 * group + 2),)),
            dma((kv, 2 + group)),
            dma((kv, 2)),
            dma((kv, 2)),
            dma,
            dma,
            dma((kv, 2, 2, 4)),
            dma((kv, 2, 2, 4)),
            dma((kv, Z)),
            dma((kv, Z)),
            dma((kv, Z)),
            dma((kv, Z)),
            dma((kv, 2, 4, 2)),
            dma((kv, 2, 4, 2)),
            dma((kv, 2)),
            dma((kv, 2)),
            dma((Z,)),
            dma((Z,)),
            dma((second,)),
            dma((second,)),
            dma((third,)),
            dma((third,)),
        ],
        compiler_params=pltpu.CompilerParams(
            collective_id=0, has_side_effects=True, vmem_limit_bytes=54784 * 1024),
    )(counts, rate_table, rate_index, queries, keys, values, grad_out)
    out = pl.pallas_call(
        placed,
        out_shape=tuple(jax.ShapeDtypeStruct(x.shape, x.dtype) for x in out),
        in_specs=[any_] * 4,
        out_specs=(any_,) * 4,
        scratch_shapes=[dma((4,))],
        compiler_params=pltpu.CompilerParams(vmem_limit_bytes=16 * 1024 * 1024),
    )(*out)
    return out[0], out[1], out[2], out[3].reshape(levels)


def solution(mesh):
    split = P("req", "ctx", "head")
    return jax.shard_map(
        shards,
        mesh=mesh,
        in_specs=(split, split, split, split, P("req"), P(), P("req", "ctx")),
        out_specs=(split, split, split, P()),
        check_vma=False,
    )
```

```python
import functools

import jax
import jax.numpy as jnp
from jax import lax
from jax.experimental import pallas as pl
from jax.experimental.pallas import tpu as pltpu
from jax.sharding import PartitionSpec as P

HD = 128
Z = 8
SCALE = 128.0 ** (-0.5)
LOG2E = 1.4426950408889634
MESH = pl.DeviceIdType.MESH
F32 = jnp.float32
BF16 = jnp.bfloat16
NT = (((1,), (1,)), ((), ()))
TN = (((0,), (0,)), ((), ()))
NN = (((1,), (0,)), ((), ()))
NEAR = (6, 2, 7, 1)
FAR = (4, 5, 3)
SHORT = (0, 1)


def kernel(
    n_head, n_req, cand, pre, group, kv, levels,
    counts_ref, table_ref, index_ref, q_hbm, k_hbm, v_hbm, o_hbm,
    dq_hbm, dk_hbm, dv_hbm, dt_ref,
    qo, ks, vs, kt, idx_par, bias, onehot,
    probs, dprobs, peaks, deltas, fin, lev_a, lev_b, st_loc, st_in, st_all,
    dq_all, rs_out, rs_in, dq_done, dk_acc, dv_acc, kv_out, kv_in, kv_done,
    t_mid, t_in1, t_in2, t_in3,
    in_sem, out_sem, kv_send, kv_recv, ix_send, ix_recv,
    ag_send, ag_recv, sa_send, sa_recv, sb_send, sb_recv,
    rs_send, rs_recv, dk_send, dk_recv,
    t1_send, t1_recv, t2_send, t2_recv, t3_send, t3_recv,
):
    rows = group * cand
    half = rows // 2
    lanes = rows // HD
    n_core = min(n_req, 2)
    n_hi = n_req // n_core
    ctx = lax.axis_index("ctx")
    head = lax.axis_index("head")
    req = lax.axis_index("req")
    y = ctx // Z
    z = ctx % Z
    hi = req // n_core
    core = req % n_core

    def along_z(by):
        return {"ctx": y * Z + (z + by) % Z}

    partner = {"ctx": (1 - y) * Z + z}
    right, left = along_z(1), along_z(Z - 1)
    far_right, far_left = along_z(2), along_z(Z - 2)
    t2_codes = [(a, b) for a in range(n_head) for b in range(n_core)][1:]
    t3_codes = [(a, b) for a in range(2) for b in range(n_hi)][1:]

    def t2_peer(a, b):
        return {"head": (head + a) % n_head, "req": hi * n_core + (core + b) % n_core}

    def t3_peer(a, b):
        return {
            "ctx": ((y + a) % 2) * Z + z, "req": ((hi + b) % n_hi) * n_core + core}

    barrier = pltpu.get_barrier_semaphore()
    peers = [left, right]
    peers += [t2_peer(*code) for code in t2_codes] + [t3_peer(*code) for code in t3_codes]
    for peer in peers:
        pl.semaphore_signal(barrier, inc=1, device_id=peer, device_id_type=MESH)

    loads, late_loads = [], []
    for g in range(kv):
        for j in range(group):
            lo = (g * group + j) * HD
            for part, src in ((0, q_hbm), (1, o_hbm)):
                loads.append(pltpu.make_async_copy(
                    src.at[0, :, pl.ds(lo, HD)],
                    qo.at[0, g, part, pl.ds(j * cand, cand), :],
                    in_sem.at[len(loads)]))
    for g in range(kv):
        for src, dst in ((k_hbm, ks), (v_hbm, vs)):
            late_loads.append(pltpu.make_async_copy(
                src.at[0, :, pl.ds(g * HD, HD)],
                dst.at[g, pl.ds(0, pre), :],
                in_sem.at[len(loads) + len(late_loads)]))
    for copy in loads + late_loads:
        copy.start()

    pl.semaphore_wait(barrier, len(peers))

    def remote(src, dst, send, recv, device):
        return pltpu.make_async_remote_copy(
            src_ref=src, dst_ref=dst, send_sem=send, recv_sem=recv,
            device_id=device, device_id_type=MESH)

    def gather(g, way, step, part):
        if way == 0:
            src, dst, device = lax.rem(9 - step, Z), Z - step, right
        else:
            src, dst, device = step - 1, step, left
        return remote(
            qo.at[src, g, part], qo.at[dst, g, part],
            ag_send.at[g, way, part, step - 1], ag_recv.at[g, way, part, step - 1], device)

    def kv_copy(g, which):
        ref = (ks, vs)[which]
        return remote(
            ref.at[g, pl.ds(0, pre), :], ref.at[g, pl.ds(pre, pre), :],
            kv_send.at[g, which], kv_recv.at[g, which], partner)

    ix_copy = remote(index_ref, idx_par, ix_send, ix_recv, partner)

    def stat_a(g, o):
        return remote(
            st_loc.at[g, o], st_in.at[g, o],
            sa_send.at[g, o], sa_recv.at[g, o], along_z(o))

    def stat_b(g, o):
        return remote(
            st_all.at[g, 0], st_all.at[g, o],
            sb_send.at[g, o], sb_recv.at[g, o], along_z(o))

    def scatter(g, way, step, part):
        at = pl.ds(part * half, half) if step == 0 else pl.ds(0, rows)
        return remote(
            rs_out.at[g, way, step, at, :], rs_in.at[g, way, step, at, :],
            rs_send.at[g, way, step, part], rs_recv.at[g, way, step, part],
            (far_left, far_right)[way] if step == 0 and g in SHORT else (left, right)[way])

    def kv_grad(g, which):
        return remote(
            kv_out.at[g, which], kv_in.at[g, which],
            dk_send.at[g, which], dk_recv.at[g, which], partner)

    def t1_copy(o):
        return remote(
            t_mid.at[0], t_in1.at[o], t1_send.at[o], t1_recv.at[o], along_z(o))

    def t2_copy(i):
        return remote(
            t_mid.at[1], t_in2.at[i], t2_send.at[i], t2_recv.at[i], t2_peer(*t2_codes[i]))

    def t3_copy(i):
        return remote(
            t_mid.at[2], t_in3.at[i], t3_send.at[i], t3_recv.at[i], t3_peer(*t3_codes[i]))

    live = counts_ref[0] - ctx * cand
    slot = lax.rem(lax.broadcasted_iota(jnp.int32, (rows, HD), 0), cand)
    for g in range(kv):
        for part in range(2):
            for j in range(group):
                loads[2 * (g * group + j) + part].wait()
            if part == 1:
                qo[0, g, 1] = jnp.where(
                    slot < live, qo[0, g, 1], jnp.zeros((rows, HD), BF16))
            for way in range(2):
                gather(g, way, 1, part).start()
    ix_copy.start()
    for g in range(kv):
        for which in range(2):
            late_loads[2 * g + which].wait()
            kv_copy(g, which).start()

    dk_acc[...] = jnp.zeros_like(dk_acc)
    dv_acc[...] = jnp.zeros_like(dv_acc)

    level = lax.broadcasted_iota(jnp.int32, (levels, HD), 0)
    table = jnp.zeros((levels, HD), F32)
    for i in range(levels):
        table = jnp.where(level == i, table_ref[i], table)
    table = table.astype(BF16)

    def offsets(index, place):
        hot = (lax.broadcasted_iota(jnp.int32, (levels, pre), 0) == index)
        hot = hot.astype(F32).astype(BF16)
        onehot[:, pl.ds(place * pre, pre)] = hot
        bias[pl.ds(place * pre, pre), :] = lax.dot_general(
            hot, table, TN, preferred_element_type=F32) * LOG2E

    offsets(index_ref[...], 0)

    def split(row):
        return [row[:, i * HD:(i + 1) * HD] for i in range(lanes)]

    def joined(block):
        return jnp.concatenate([block[i:i + 1] for i in range(lanes)], axis=1)

    def first_pass(g, s):
        q_blk = qo[s, g, 0]
        o_blk = qo[s, g, 1]
        off = jnp.concatenate([bias[...]] * lanes, axis=1)
        scores = lax.dot_general(ks[g], q_blk, NT, preferred_element_type=F32)
        scores = scores * (SCALE * LOG2E) + off
        peak = jnp.max(scores, axis=0, keepdims=True)
        prob = jnp.exp2(scores - peak)
        total = jnp.sum(prob, axis=0, keepdims=True)
        dprob = lax.dot_general(vs[g], o_blk, NT, preferred_element_type=F32)
        delta = jnp.sum(prob * dprob, axis=0, keepdims=True) / total
        probs[g, s] = prob
        dprobs[g, s] = dprob
        peaks[g, s] = peak
        deltas[g, s] = delta
        lev_a[g, s] = lax.dot_general(
            onehot[...], (prob * (dprob - delta)).astype(BF16), NN,
            preferred_element_type=F32)
        lev_b[g, s] = lax.dot_general(
            onehot[...], prob.astype(BF16), NN, preferred_element_type=F32)
        lse = peak + jnp.log2(total)
        st_loc[g, s] = jnp.concatenate(split(lse) + split(delta), axis=0)

    def merged(parts):
        lse = [p[0:lanes] for p in parts]
        top = functools.reduce(jnp.maximum, lse)
        total = top + jnp.log2(sum(jnp.exp2(v - top) for v in lse))
        delta = sum(jnp.exp2(v - total) * p[lanes:] for v, p in zip(lse, parts))
        return total, delta

    def combine(g):
        total, delta = merged([st_loc[g, 0]] + [st_in[g, o] for o in NEAR])
        st_all[g, 0, 0] = jnp.concatenate([total, delta], axis=0)

    def finish(g):
        acc = []
        for s in range(Z):
            total, delta = merged([st_all[g, (Z - s) % Z, 0]] + [
                st_all[g, (Z + o - s) % Z, 1 + i] for i, o in enumerate(FAR)])
            delta = joined(delta)
            factor = jnp.exp2(peaks[g, s] - joined(total))
            fin[g, s] = jnp.concatenate([factor, delta], axis=0)
            term = factor * (lev_a[g, s] - (delta - deltas[g, s]) * lev_b[g, s])
            acc += split(term)
        return sum(acc)

    def second_pass(g, s):
        both = fin[g, s]
        prob = probs[g, s] * both[0:1]
        dscore = prob * (dprobs[g, s] - both[1:2])
        prob_b = prob.astype(BF16)
        dscore_b = dscore.astype(BF16)
        dq = lax.dot_general(kt[g], dscore_b, NN, preferred_element_type=F32)
        dq_all[g, s] = dq.T
        dv_acc[g] += lax.dot_general(prob_b, qo[s, g, 1], NN, preferred_element_type=F32)
        dk_acc[g] += lax.dot_general(dscore_b, qo[s, g, 0], NN, preferred_element_type=F32)

    def kv_finish(g):
        for which, acc in ((0, dk_acc), (1, dv_acc)):
            kv_grad(g, which).wait_recv()
            total = acc[g, 0:pre] + kv_in[g, which].astype(F32)
            if which == 0:
                total = total * SCALE
            kv_done[g, which] = total.astype(BF16)
            kv_store(g, which).start()

    def kv_store(g, which):
        hbm = (dk_hbm, dv_hbm)[which]
        return pltpu.make_async_copy(
            kv_done.at[g, which], hbm.at[0, :, pl.ds(g * HD, HD)], out_sem.at[g, which])

    def dq_store(g, j):
        return pltpu.make_async_copy(
            dq_done.at[g, pl.ds(j * cand, cand), :],
            dq_hbm.at[0, :, pl.ds((g * group + j) * HD, HD)],
            out_sem.at[g, 2 + j])

    def gather_tick(t, _):
        k, g = 1 + t // kv, t % kv

        @pl.when(k < 4)
        def _():
            for part in range(2):
                for way in range(2):
                    gather(g, way, k, part).wait_recv()

                    @pl.when((k < 3) | (part == way))
                    def _():
                        gather(g, way, k + 1, part).start()

        @pl.when(k == 4)
        def _():
            for o in NEAR:
                stat_a(g, o).wait()
            combine(g)
            gather(g, 0, 4, 0).wait_recv()
            gather(g, 1, 4, 1).wait_recv()

        for i in range(kv):
            @pl.when((k == 1) & (g == i))
            def _():
                if i == 0:
                    ix_copy.wait()
                    offsets(idx_par[...], 1)
                for which in range(2):
                    kv_copy(i, which).wait()
                kt[i] = ks[i].astype(F32).T.astype(BF16)

        def chunk(c, _):
            first_pass(g, jnp.where(c == 0, Z - k, jnp.where(c == 1, k, 0)))
            return 0

        lax.fori_loop(0, jnp.where(k == 4, 1, jnp.where(k == 1, 3, 2)), chunk, 0)

        @pl.when(k == 2)
        def _():
            for o in NEAR:
                stat_a(g, o).start()

        @pl.when(k == 4)
        def _():
            for i, o in enumerate(FAR):
                st_all[g, 0, 1 + i] = st_loc[g, o]
            for o in (4, 5, 3, 6, 2, 7, 1):
                stat_b(g, o).start()

        return 0

    lax.fori_loop(0, 4 * kv, gather_tick, 0)

    def stats(g):
        for o in (1, 7, 2, 6, 3, 5, 4):
            stat_b(g, o).wait()
        term = finish(g)
        place = lax.broadcasted_iota(jnp.int32, (levels, HD), 0)
        across = lax.broadcasted_iota(jnp.int32, (levels, HD), 1)
        term = jnp.sum(term, axis=1, keepdims=True)
        term = jnp.sum(jnp.where(place == across, term, 0.0), axis=0, keepdims=True)
        t_mid[0] = term if g == 0 else t_mid[0] + term

    def table_first():
        for o in range(1, Z):
            t1_copy(o).start()

    def table_second():
        for o in range(1, Z):
            t1_copy(o).wait()
        t_mid[1] = t_mid[0] + sum(t_in1[o] for o in range(1, Z))
        for i in range(len(t2_codes)):
            t2_copy(i).start()

    def table_third():
        for i in range(len(t2_codes)):
            t2_copy(i).wait()
        t_mid[2] = t_mid[1] + sum(t_in2[i] for i in range(len(t2_codes)))
        for i in range(len(t3_codes)):
            t3_copy(i).start()

    def scatter_first(g):
        for way in range(2):
            at = pl.ds(way * half, half)
            rs_out[g, way, 0, at, :] = dq_all[g, 4, at, :].astype(BF16)
            scatter(g, way, 0, way).start()

    def scatter_next(g, step):
        for way in range(2):
            dq = dq_all[g, 4 + step if way == 0 else 4 - step]
            if step > 1:
                scatter(g, way, step - 1, 0).wait_recv()
                dq = dq + rs_in[g, way, step - 1].astype(F32)
            rs_out[g, way, step] = dq.astype(BF16)
            if step == 2:
                scatter(g, way, 0, way).wait_recv()
                at = pl.ds(way * half, half)
                dq = dq_all[g, 4 + step if way == 0 else 4 - step, at, :]
                dq = dq + rs_in[g, way, 1, at, :].astype(F32) + rs_in[g, way, 0, at, :].astype(F32)
                rs_out[g, way, step, at, :] = dq.astype(BF16)
            scatter(g, way, step, 0).start()

    def scatter_last(g):
        for way in range(2):
            scatter(g, way, 3, 0).wait_recv()
        dq = dq_all[g, 0] + rs_in[g, 0, 3].astype(F32) + rs_in[g, 1, 3].astype(F32)
        dq_done[g] = (dq * SCALE).astype(BF16)
        for j in range(group):
            dq_store(g, j).start()

    def kv_send_off(g):
        for which, acc in ((0, dk_acc), (1, dv_acc)):
            kv_out[g, which] = acc[g, pre:2 * pre].astype(BF16)
            kv_grad(g, which).start()

    order = [(0, 4), (0, 5), (0, 3), (1, 4), (1, 5), (1, 3), (0, 6), (0, 2), (1, 6), (1, 2),
             (0, 7), (0, 1), (0, 0), (1, 7), (1, 1), (1, 0)]
    before = {0: [lambda: stats(0)], 3: [lambda: stats(1), table_first]}
    after = {
        0: [lambda: scatter_first(0)],
        2: [lambda: scatter_next(0, 1)],
        3: [lambda: scatter_first(1)],
        5: [lambda: scatter_next(1, 1)],
        11: [lambda: scatter_next(0, 2)],
        12: [lambda: kv_send_off(0)],
        14: [lambda: scatter_next(1, 2), table_second],
        15: [lambda: kv_send_off(1)],
    }

    def grad_tick(e, _):
        for at, calls in before.items():
            @pl.when(e == at)
            def _():
                for call in calls:
                    call()

        g = jnp.int32(0)
        s = jnp.int32(0)
        for i, (a, b) in enumerate(order):
            g = jnp.where(e == i, a, g)
            s = jnp.where(e == i, b, s)
        second_pass(g, s)

        for at, calls in after.items():
            @pl.when(e == at)
            def _():
                for call in calls:
                    call()
        return 0

    lax.fori_loop(0, len(order), grad_tick, 0)

    scatter_next(0, 3)
    scatter_next(1, 3)
    table_third()
    kv_finish(0)
    scatter_last(0)

    for g in range(kv):
        for way in range(2):
            for part in range(2):
                for step in range(1, 5):
                    if step < 4 or part == way:
                        gather(g, way, step, part).wait_send()
                for step in range(4):
                    if part == (0 if step > 0 else way):
                        scatter(g, way, step, part).wait_send()
        for which in range(2):
            kv_grad(g, which).wait_send()

    kv_finish(1)
    scatter_last(1)
    for i in range(len(t3_codes)):
        t3_copy(i).wait()
    total = t_mid[2] + sum(t_in3[i] for i in range(len(t3_codes)))
    dt_ref[...] = total[:, 0:levels]

    for g in range(kv):
        for which in range(2):
            kv_store(g, which).wait()
        for j in range(group):
            dq_store(g, j).wait()


def placed(*refs):
    copies = [
        pltpu.make_async_copy(refs[i], refs[4 + i], refs[8].at[i]) for i in range(4)]
    for copy in copies:
        copy.start()
    for copy in copies:
        copy.wait()


def shards(queries, keys, values, grad_out, counts, rate_table, rate_index):
    n_head, n_req = lax.axis_size("head"), lax.axis_size("req")
    cand, pre = queries.shape[1], keys.shape[1]
    kv = keys.shape[2] // HD
    group = queries.shape[2] // keys.shape[2]
    levels = rate_table.shape[0]
    rows = group * cand
    lanes = rows // HD
    second = max(n_head * min(n_req, 2) - 1, 1)
    third = 2 * (n_req // min(n_req, 2)) - 1
    any_ = pl.BlockSpec(memory_space=pl.ANY)
    smem = pl.BlockSpec(memory_space=pltpu.SMEM)
    vmem = pl.BlockSpec(memory_space=pltpu.VMEM)
    dma = pltpu.SemaphoreType.DMA
    out = pl.pallas_call(
        functools.partial(kernel, n_head, n_req, cand, pre, group, kv, levels),
        out_shape=(
            jax.ShapeDtypeStruct(queries.shape, BF16),
            jax.ShapeDtypeStruct(keys.shape, BF16),
            jax.ShapeDtypeStruct(values.shape, BF16),
            jax.ShapeDtypeStruct((1, levels), F32),
        ),
        in_specs=[smem, smem, vmem, any_, any_, any_, any_],
        out_specs=(any_, any_, any_, vmem),
        scratch_shapes=[
            pltpu.VMEM((Z, kv, 2, rows, HD), BF16),
            pltpu.VMEM((kv, 2 * pre, HD), BF16),
            pltpu.VMEM((kv, 2 * pre, HD), BF16),
            pltpu.VMEM((kv, HD, 2 * pre), BF16),
            pltpu.VMEM((1, pre), jnp.int32),
            pltpu.VMEM((2 * pre, HD), F32),
            pltpu.VMEM((levels, 2 * pre), BF16),
            pltpu.VMEM((kv, Z, 2 * pre, rows), F32),
            pltpu.VMEM((kv, Z, 2 * pre, rows), F32),
            pltpu.VMEM((kv, Z, 1, rows), F32),
            pltpu.VMEM((kv, Z, 1, rows), F32),
            pltpu.VMEM((kv, Z, 2, rows), F32),
            pltpu.VMEM((kv, Z, levels, rows), F32),
            pltpu.VMEM((kv, Z, levels, rows), F32),
            pltpu.VMEM((kv, Z, 2 * lanes, HD), F32),
            pltpu.VMEM((kv, Z, 2 * lanes, HD), F32),
            pltpu.VMEM((kv, Z, 4, 2 * lanes, HD), F32),
            pltpu.VMEM((kv, Z, rows, HD), F32),
            pltpu.VMEM((kv, 2, 4, rows, HD), BF16),
            pltpu.VMEM((kv, 2, 4, rows, HD), BF16),
            pltpu.VMEM((kv, rows, HD), BF16),
            pltpu.VMEM((kv, 2 * pre, HD), F32),
            pltpu.VMEM((kv, 2 * pre, HD), F32),
            pltpu.VMEM((kv, 2, pre, HD), BF16),
            pltpu.VMEM((kv, 2, pre, HD), BF16),
            pltpu.VMEM((kv, 2, pre, HD), BF16),
            pltpu.VMEM((3, 1, HD), F32),
            pltpu.VMEM((Z, 1, HD), F32),
            pltpu.VMEM((second, 1, HD), F32),
            pltpu.VMEM((third, 1, HD), F32),
            dma((kv * (2 * group + 2),)),
            dma((kv, 2 + group)),
            dma((kv, 2)),
            dma((kv, 2)),
            dma,
            dma,
            dma((kv, 2, 2, 4)),
            dma((kv, 2, 2, 4)),
            dma((kv, Z)),
            dma((kv, Z)),
            dma((kv, Z)),
            dma((kv, Z)),
            dma((kv, 2, 4, 2)),
            dma((kv, 2, 4, 2)),
            dma((kv, 2)),
            dma((kv, 2)),
            dma((Z,)),
            dma((Z,)),
            dma((second,)),
            dma((second,)),
            dma((third,)),
            dma((third,)),
        ],
        compiler_params=pltpu.CompilerParams(
            collective_id=0, has_side_effects=True, vmem_limit_bytes=54784 * 1024),
    )(counts, rate_table, rate_index, queries, keys, values, grad_out)
    out = pl.pallas_call(
        placed,
        out_shape=tuple(jax.ShapeDtypeStruct(x.shape, x.dtype) for x in out),
        in_specs=[any_] * 4,
        out_specs=(any_,) * 4,
        scratch_shapes=[dma((4,))],
        compiler_params=pltpu.CompilerParams(vmem_limit_bytes=16 * 1024 * 1024),
    )(*out)
    return out[0], out[1], out[2], out[3].reshape(levels)


def solution(mesh):
    split = P("req", "ctx", "head")
    return jax.shard_map(
        shards,
        mesh=mesh,
        in_specs=(split, split, split, split, P("req"), P(), P("req", "ctx")),
        out_specs=(split, split, split, P()),
        check_vma=False,
    )
```
